32 devices in a mesh: groups: 2 (over x), inner: 16 (over z, y, core).
Axes of the slice: x: 2, y: 2, z: 4, core: 2. Of those that a mesh axis runs over, the one named last changes fastest.
Arguments:
- hidden_rows: bfloat16 [2048, 2048], P(('groups', 'inner')), parts along dimension 0, may hold values from -6 to 6
- token_embed: bfloat16 [2048, 2048], P(('groups', 'inner')), parts along dimension 0, may hold values from -6 to 6
- first_routes: int32 [2048, 8], P(('groups', 'inner')), parts along dimension 0, may hold values from 0 to 15, all different within a row; in each aligned block of 64 rows (0 to 63, 64 to 127, ...) at most 48 rows name the same one
- first_gates: float32 [2048, 8], P(('groups', 'inner')), parts along dimension 0, may hold values from 0.2 to 0.6
- first_gate_up: bfloat16 [16, 2048, 1024], P('inner'), may hold values from -0.125 to 0.125
- first_down: bfloat16 [16, 512, 2048], P('inner'), may hold values from -0.25 to 0.25
- second_routes: int32 [2048, 8], P(('groups', 'inner')), parts along dimension 0, may hold values from 0 to 15, all different within a row; in each aligned block of 64 rows (0 to 63, 64 to 127, ...) at most 48 rows name the same one
- second_gates: float32 [2048, 8], P(('groups', 'inner')), parts along dimension 0, may hold values from 0.2 to 0.6
- second_gate_up: bfloat16 [16, 2048, 1024], P('inner'), may hold values from -0.125 to 0.125
- second_down: bfloat16 [16, 512, 2048], P('inner'), may hold values from -0.25 to 0.25
- hidden_gain: float32 [2048], replicated, may hold values from 0.25 to 1.75
- embed_gain: float32 [2048], replicated, may hold values from 0.25 to 1.75
- merge_weight: bfloat16 [4096, 2048], P('inner'), may hold values from -0.09375 to 0.09375
Outputs:
- final_rows: bfloat16 [2048, 2048], P(('groups', 'inner')), parts along dimension 0
The draws below stay inside these ranges and needn't reach their ends.
There are 2 independent parts, one for each index of `groups`. The reference program is written for one: setup_inputs(seed, part) draws one part's arguments, and reference() takes and returns one part's arrays. A program takes and returns all parts, laid end to end along the dimension named above; an argument that names none is the same for every part. Nothing has to cross between parts.
Inputs may be any that keep to these rules, and one draw needn't show every extreme that they name: `first_routes`: among the 64 tokens of one block, no expert is named more than 48 times, and in every draw some expert is named exactly 48 times in some block. `second_routes`: among the 64 tokens of one block, no expert is named more than 48 times, and in every draw some expert is named exactly 48 times in some block.
All inputs are finite; a program needn't handle non-finite values.
Results may differ from the reference program's by a relative error of at most 0.01.
Values may be sent and summed in bfloat16 or wider, within the bound.
No kernel may reach another device: no remote copies, remote signals or barrier semaphores. Data moves between devices by JAX's collectives and lax.ppermute only.
A program may use at most 128 MiB of HBM per device.

```python
import math
import jax
import jax.numpy as jnp
import numpy as np
from jax import lax

D = 2048
FFW = 512
TOP = 8
TOK_DEV = 64
EXPERTS = 16
TOKENS = 1024
CAP = 48
N_INNER = 16


def block_scale(key, extent, pieces, low, top_value):
    def one(axis_at, blocks):
        steps = jax.random.uniform(jax.random.fold_in(jax.random.fold_in(key, 6), axis_at), (blocks,), jnp.float32, low / len(pieces), top_value / len(pieces))
        return jnp.repeat(jnp.exp(steps), extent[axis_at] // blocks).reshape((-1,) + (1,) * (len(extent) - axis_at - 1))

    loudness = one(*pieces[0])
    for cut in pieces[1:]:
        loudness = loudness * one(*cut)
    return loudness


def deal_out(rng, own, number, rows, count, top, most, skew):
    order = jax.random.permutation(rng, count)
    heavy_load, usual = shares(count, rows * top, most, skew, True), shares(count, rows * top, most, skew, False)
    places = jnp.arange(count)

    def named(tallies, turn):
        used = int((tallies > 0).sum())
        fixed = max(1, used // 4)
        passed = fixed + (places - fixed + turn * (used - fixed)) % max(1, count - fixed)
        return jnp.zeros((count,), jnp.int32).at[order[jnp.where(places < fixed, places, passed)]].set(jnp.asarray(tallies, jnp.int32))

    tallies = jnp.where(number % 4 == 0, named(heavy_load, number // 4), named(usual, number - number // 4 - 1))
    mixed = jax.random.permutation(jax.random.fold_in(own, 3), count)
    giver, receiver = mixed[0:count // 2 * 2:2], mixed[1:count // 2 * 2:2]
    slack = jnp.minimum(tallies[giver] - 1, most - tallies[receiver]) // 2
    slack = jnp.where((giver == order[0]) | (receiver == order[0]) | (tallies[receiver] == 0), 0, jnp.maximum(slack, 0))
    passed = jax.random.randint(jax.random.fold_in(own, 4), (count // 2,), 0, 1 << 20) % (slack + 1)
    tallies = tallies.at[giver].add(-passed).at[receiver].add(passed)
    labels = jnp.searchsorted(jnp.cumsum(tallies), jnp.arange(rows * top), side="right").astype(jnp.int32)
    listing = labels.reshape(top, rows).T
    listing = listing[jax.random.permutation(jax.random.fold_in(own, 1), rows)]
    turn = jax.random.randint(jax.random.fold_in(own, 2), (rows, 1), 0, top)
    return jnp.take_along_axis(listing, (jnp.arange(top)[None, :] + turn) % top, axis=1)


def shares(amount, total, limit, slope, full):
    weights = [(1 << 20) // math.isqrt(rank ** slope) + 1 for rank in range(1, amount + 1)]
    largest = limit if full else min(limit, max(-(-total // amount), total * weights[0] // sum(weights)))
    least = 1 if total - largest >= amount - 1 else 0
    holding, spare = [largest] + [least] * (amount - 1), total - largest - least * (amount - 1)
    while spare > 0:
        candidates = [i for i in range(1, amount) if holding[i] < largest] or [i for i in range(1, amount) if holding[i] < limit]
        whole, budget = sum([weights[i] for i in candidates]), spare
        for i in candidates:
            more = min(limit - holding[i], max(1, budget * weights[i] // whole), spare)
            holding[i] = holding[i] + more
            spare = spare - more
    return np.array(holding)


def bell_draw(own_key, extent, spread, reach, cuts=(), held_as=jnp.bfloat16):
    values = jax.random.normal(own_key, extent, jnp.float32) * spread
    if len(cuts) > 0:
        values = block_scale(own_key, extent, cuts, -0.22, 0.18) * values
    return jnp.clip(values, min=-reach, max=reach).astype(held_as)


def setup_inputs(seed: int = 0, part: int = 0) -> dict:
    key_of = jax.random.split(jax.random.key(seed), 14)
    part_splits = jax.random.split(jax.random.fold_in(key_of[13], part), 14)
    hidden_rows = bell_draw(part_splits[0], (TOKENS, D), 1.0, 6.0, ((0, 16),))
    token_embed = bell_draw(part_splits[1], (TOKENS, D), 1.0, 6.0, ((0, 16),))
    first_routes_keys = jax.random.split(jax.random.fold_in(part_splits[2], 1), TOKENS // TOK_DEV)
    first_routes_turns = jax.random.permutation(jax.random.fold_in(part_splits[2], 3), TOKENS // TOK_DEV)
    first_routes = jax.vmap(lambda own, number: deal_out(jax.random.fold_in(part_splits[2], 2), own, number, TOK_DEV, EXPERTS, TOP, CAP, 2))(first_routes_keys, first_routes_turns).reshape((TOKENS, TOP))
    first_gates = jnp.clip(0.2 + 0.400000021 * jax.random.uniform(part_splits[3], (TOKENS, TOP), jnp.float32) ** block_scale(part_splits[3], (TOKENS, TOP), ((0, 16),), -0.2, 0.2), 0.2, 0.6)
    first_gate_up = bell_draw(key_of[4], (EXPERTS, D, 2 * FFW), D ** -0.5, 0.125, ((0, 16),))
    first_down = bell_draw(key_of[5], (EXPERTS, FFW, D), FFW ** -0.5, 0.25, ((0, 16),))
    second_routes_keys = jax.random.split(jax.random.fold_in(part_splits[6], 1), TOKENS // TOK_DEV)
    second_routes_turns = jax.random.permutation(jax.random.fold_in(part_splits[6], 3), TOKENS // TOK_DEV)
    second_routes = jax.vmap(lambda own, number: deal_out(jax.random.fold_in(part_splits[6], 2), own, number, TOK_DEV, EXPERTS, TOP, CAP, 1))(second_routes_keys, second_routes_turns).reshape((TOKENS, TOP))
    second_gates = jnp.clip(0.2 + 0.400000021 * jax.random.uniform(part_splits[7], (TOKENS, TOP), jnp.float32) ** block_scale(part_splits[7], (TOKENS, TOP), ((0, 16),), -0.2, 0.2), 0.2, 0.6)
    second_gate_up = bell_draw(key_of[8], (EXPERTS, D, 2 * FFW), D ** -0.5, 0.125, ((0, 16),))
    second_down = bell_draw(key_of[9], (EXPERTS, FFW, D), FFW ** -0.5, 0.25, ((0, 16),))
    hidden_gain = jnp.clip(1.0 + 0.15 * jax.random.normal(key_of[10], (D,), jnp.float32), 0.25, 1.75)
    embed_gain = jnp.clip(1.0 + 0.15 * jax.random.normal(key_of[11], (D,), jnp.float32), 0.25, 1.75)
    merge_weight = bell_draw(key_of[12], (2 * D, D), (2 * D) ** -0.5, 0.09375, ((0, 16),))
    return dict(hidden_rows=hidden_rows, token_embed=token_embed, first_routes=first_routes, first_gates=first_gates, first_gate_up=first_gate_up, first_down=first_down, second_routes=second_routes, second_gates=second_gates, second_gate_up=second_gate_up, second_down=second_down, hidden_gain=hidden_gain, embed_gain=embed_gain, merge_weight=merge_weight)


EPSILON = 1e-06

def expert_apply(slot_rows, expert_gu, expert_down):
    inner_width = expert_down.shape[0]
    projected = jnp.dot(slot_rows, expert_gu, preferred_element_type=jnp.float32)
    inner = (jax.nn.silu(projected[:, :inner_width]) * projected[:, inner_width:]).astype(jnp.bfloat16)
    return jnp.dot(inner, expert_down, preferred_element_type=jnp.float32).astype(jnp.bfloat16)

def rms_scale(values, gain_vec):
    widened = values.astype(jnp.float32)
    inverse_rms = lax.rsqrt(lax.optimization_barrier(jnp.mean(widened * widened, axis=-1, keepdims=True)) + EPSILON)
    return (widened * inverse_rms * gain_vec.astype(jnp.float32)).astype(jnp.bfloat16)

def routed_reference(inputs, routes, weights_in, gate_up, down_proj):
    tokens_all, feature_dim = inputs.shape
    top_count = routes.shape[1]
    experts = gate_up.shape[0]
    blocks = N_INNER
    per_block = tokens_all // blocks
    capacity = max(2, 3 * per_block * top_count // (2 * experts))
    grouped = routes.reshape(blocks, per_block * top_count)
    onehot = (grouped[:, :, None] == jnp.arange(experts, dtype=jnp.int32)[None, None, :]).astype(jnp.int32)
    ranking = lax.optimization_barrier(jnp.sum(onehot * (jnp.cumsum(onehot, axis=1) - 1), axis=2))
    source = jnp.arange(blocks, dtype=jnp.int32)[:, None] * capacity
    position = (grouped * (blocks * capacity) + source + ranking).reshape(-1).astype(jnp.int32)
    repeated = jnp.repeat(inputs, top_count, axis=0)
    buffer_rows = jnp.zeros((experts * blocks * capacity, feature_dim), jnp.bfloat16).at[position].set(repeated)

    def one_expert(operands):
        slot_rows, expert_gu, expert_down = operands
        return expert_apply(slot_rows, expert_gu, expert_down)
    outputs = lax.map(one_expert, (buffer_rows.reshape(experts, blocks * capacity, feature_dim), gate_up, down_proj))
    picked = outputs.reshape(-1, feature_dim)[position].reshape(tokens_all, top_count, feature_dim)
    return lax.optimization_barrier(jnp.sum(picked.astype(jnp.float32) * weights_in.astype(jnp.float32)[:, :, None], axis=1))

def reference(hidden_rows, token_embed, first_routes, first_gates, first_gate_up, first_down, second_routes, second_gates, second_gate_up, second_down, hidden_gain, embed_gain, merge_weight):
    first_moe = routed_reference(hidden_rows, first_routes, first_gates, first_gate_up, first_down)
    after_first = (hidden_rows.astype(jnp.float32) + first_moe).astype(jnp.bfloat16)
    merged_in = jnp.concatenate([rms_scale(after_first, hidden_gain), rms_scale(token_embed, embed_gain)], axis=1)
    merged = jnp.dot(merged_in, merge_weight, preferred_element_type=jnp.float32)
    after_merge = (after_first.astype(jnp.float32) + jax.nn.silu(merged)).astype(jnp.bfloat16)
    second_moe = routed_reference(after_merge, second_routes, second_gates, second_gate_up, second_down)
    return (after_merge.astype(jnp.float32) + second_moe).astype(jnp.bfloat16)
```

```python
import jax
import jax.numpy as jnp
from jax import lax
from jax.sharding import PartitionSpec as P

EPSILON = 1e-06


def gate_table(routes, gates, experts):
    named = routes[:, :, None] == jnp.arange(experts, dtype=jnp.int32)[None, None, :]
    return jnp.sum(jnp.where(named, gates[:, :, None], 0.0), axis=1)


def normed(values, gain):
    widened = values.astype(jnp.float32)
    inverse = lax.rsqrt(jnp.mean(widened * widened, axis=-1, keepdims=True) + EPSILON)
    return (widened * inverse * gain).astype(jnp.bfloat16)


def expert(rows, gate_column, gate_up, down):
    width = down.shape[0]
    projected = jnp.dot(rows, gate_up, preferred_element_type=jnp.float32)
    hidden = (jax.nn.silu(projected[:, :width]) * projected[:, width:]).astype(jnp.bfloat16)
    out = jnp.dot(hidden, down, preferred_element_type=jnp.float32)
    return (out * gate_column).astype(jnp.bfloat16)


def routed(rows, gate_column, gate_up, down):
    every = lax.all_gather(rows, "inner", axis=0, tiled=True)
    part = expert(every, gate_column, gate_up, down)
    return lax.psum_scatter(part, "inner", scatter_dimension=0, tiled=True)


def local(
    hidden_rows,
    token_embed,
    first_routes,
    first_gates,
    first_gate_up,
    first_down,
    second_routes,
    second_gates,
    second_gate_up,
    second_down,
    hidden_gain,
    embed_gain,
    merge_weight,
):
    experts = lax.axis_size("inner")
    tables = jnp.stack(
        [gate_table(first_routes, first_gates, experts), gate_table(second_routes, second_gates, experts)], axis=1
    )
    columns = lax.all_to_all(tables, "inner", split_axis=2, concat_axis=0, tiled=True)
    first = routed(hidden_rows, columns[:, 0], first_gate_up[0], first_down[0])
    after_first = (hidden_rows.astype(jnp.float32) + first.astype(jnp.float32)).astype(jnp.bfloat16)
    merged_in = jnp.concatenate([normed(after_first, hidden_gain), normed(token_embed, embed_gain)], axis=1)
    slices = lax.all_to_all(merged_in, "inner", split_axis=1, concat_axis=0, tiled=True)
    partial = jnp.dot(slices, merge_weight, preferred_element_type=jnp.float32).astype(jnp.bfloat16)
    merged = lax.psum_scatter(partial, "inner", scatter_dimension=0, tiled=True).astype(jnp.float32)
    after_merge = (after_first.astype(jnp.float32) + jax.nn.silu(merged)).astype(jnp.bfloat16)
    second = routed(after_merge, columns[:, 1], second_gate_up[0], second_down[0])
    return (after_merge.astype(jnp.float32) + second.astype(jnp.float32)).astype(jnp.bfloat16)


def solution(mesh):
    rows = P(("groups", "inner"), None)
    weight = P("inner", None, None)
    return jax.shard_map(
        local,
        mesh=mesh,
        in_specs=(rows, rows, rows, rows, weight, weight, rows, rows, weight, weight, P(), P(), P("inner", None)),
        out_specs=rows,
        check_vma=False,
    )
```

```python
import jax
import jax.numpy as jnp
from jax import lax
from jax.sharding import PartitionSpec as P

EPSILON = 1e-06
PLANE = 4


class Ring:
    def __init__(self):
        self.size = lax.axis_size("inner")
        self.planes = self.size // PLANE
        self.me = lax.axis_index("inner")
        self.z = self.me // PLANE
        self.y = (self.me // 2) % 2
        self.core = self.me % 2

    def along_z(self, values, step):
        perm = [(d, (d + step * PLANE) % self.size) for d in range(self.size)]
        return lax.ppermute(values, "inner", perm)

    def across_y(self, values):
        return lax.ppermute(values, "inner", [(d, d ^ 2) for d in range(self.size)])

    def across_core(self, values):
        return lax.ppermute(values, "inner", [(d, d ^ 1) for d in range(self.size)])


def add(left, right):
    return (left.astype(jnp.float32) + right.astype(jnp.float32)).astype(jnp.bfloat16)


def gather_rows(ring, rows):
    columns = [rows if k == 0 else ring.along_z(rows, k) for k in range(ring.planes)]
    halves = [jnp.concatenate([c, ring.across_y(c)], axis=0) for c in columns]
    return [jnp.concatenate([h, ring.across_core(h)], axis=0) for h in halves]


def scatter_sum(ring, chunks):
    rows = chunks[0].shape[0] // PLANE
    total = None
    for k in range(ring.planes - 1, -1, -1):
        chunk = chunks[k]
        half = add(chunk[: 2 * rows], ring.across_core(chunk[2 * rows :]))
        part = add(half[:rows], ring.across_y(half[rows:]))
        if k:
            part = ring.along_z(part, -k)
        part = part.astype(jnp.float32)
        total = part if total is None else total + part
    return total


def gate_table(routes, gates, experts):
    named = routes[:, :, None] == jnp.arange(experts, dtype=jnp.int32)[None, None, :]
    return jnp.sum(jnp.where(named, gates[:, :, None], 0.0), axis=1)


def gate_columns(ring, tables):
    layers, rows, experts = tables.shape
    every = lax.all_gather(tables, "inner", axis=0)
    mine = lax.dynamic_index_in_dim(every, ring.me, axis=3, keepdims=False)
    step = jnp.arange(ring.planes, dtype=jnp.int32)[:, None, None]
    core = jnp.arange(2, dtype=jnp.int32)[None, :, None]
    y = jnp.arange(2, dtype=jnp.int32)[None, None, :]
    source = ((ring.z - step) % ring.planes) * PLANE + (ring.y ^ y) * 2 + (ring.core ^ core)
    return jnp.take(mine, source.reshape(-1), axis=0).transpose(1, 0, 2).reshape(layers, ring.planes, PLANE * rows, 1)


def normed(values, gain):
    widened = values.astype(jnp.float32)
    inverse = lax.rsqrt(jnp.mean(widened * widened, axis=-1, keepdims=True) + EPSILON)
    return (widened * inverse * gain).astype(jnp.bfloat16)


def expert(rows, gate_column, gate_up, down):
    width = down.shape[0]
    projected = jnp.dot(rows, gate_up, preferred_element_type=jnp.float32)
    hidden = (jax.nn.silu(projected[:, :width]) * projected[:, width:]).astype(jnp.bfloat16)
    out = jnp.dot(hidden, down, preferred_element_type=jnp.float32)
    return (out * gate_column).astype(jnp.bfloat16)


def routed(ring, rows, columns, gate_up, down):
    chunks = gather_rows(ring, rows)
    return scatter_sum(ring, [expert(c, columns[k], gate_up, down) for k, c in enumerate(chunks)])


def plane_weight(ring, weight):
    pair = jnp.concatenate([weight, ring.across_y(weight)], axis=0)
    return jnp.concatenate([pair, ring.across_core(pair)], axis=0)


def merge(ring, merged_in, weight):
    rows, features = merged_in.shape
    blocks = merged_in.reshape(rows, ring.planes, 2, 2, features // ring.size)
    blocks = jnp.where(ring.y == 1, blocks[:, :, ::-1], blocks)
    blocks = jnp.where(ring.core == 1, blocks[:, :, :, ::-1], blocks)
    by_plane = blocks.transpose(1, 0, 3, 2, 4).reshape(ring.planes, rows, features // ring.planes)
    slices = []
    for k in range(ring.planes):
        piece = lax.dynamic_index_in_dim(by_plane, (ring.z + k) % ring.planes, axis=0, keepdims=False)
        slices.append(ring.along_z(piece, k) if k else piece)
    partial = jnp.dot(jnp.concatenate(slices, axis=0), weight, preferred_element_type=jnp.float32)
    total = partial[:rows]
    for k in range(1, ring.planes):
        part = partial[k * rows : (k + 1) * rows].astype(jnp.bfloat16)
        total = total + ring.along_z(part, -k).astype(jnp.float32)
    return total


def local(
    hidden_rows,
    token_embed,
    first_routes,
    first_gates,
    first_gate_up,
    first_down,
    second_routes,
    second_gates,
    second_gate_up,
    second_down,
    hidden_gain,
    embed_gain,
    merge_weight,
):
    ring = Ring()
    tables = jnp.stack(
        [gate_table(first_routes, first_gates, ring.size), gate_table(second_routes, second_gates, ring.size)]
    )
    columns = gate_columns(ring, tables)
    weight = plane_weight(ring, merge_weight)
    first = routed(ring, hidden_rows, columns[0], first_gate_up[0], first_down[0])
    after_first = (hidden_rows.astype(jnp.float32) + first).astype(jnp.bfloat16)
    merged_in = jnp.concatenate([normed(after_first, hidden_gain), normed(token_embed, embed_gain)], axis=1)
    merged = merge(ring, merged_in, weight)
    after_merge = (after_first.astype(jnp.float32) + jax.nn.silu(merged)).astype(jnp.bfloat16)
    second = routed(ring, after_merge, columns[1], second_gate_up[0], second_down[0])
    return (after_merge.astype(jnp.float32) + second).astype(jnp.bfloat16)


def solution(mesh):
    rows = P(("groups", "inner"), None)
    weight = P("inner", None, None)
    return jax.shard_map(
        local,
        mesh=mesh,
        in_specs=(rows, rows, rows, rows, weight, weight, rows, rows, weight, weight, P(), P(), P("inner", None)),
        out_specs=rows,
        check_vma=False,
    )
```

```python
import jax
import jax.numpy as jnp
from jax import lax
from jax.sharding import PartitionSpec as P

EPSILON = 1e-06
PLANE = 4


class Ring:
    def __init__(self):
        self.size = lax.axis_size("inner")
        self.planes = self.size // PLANE
        self.me = lax.axis_index("inner")
        self.z = self.me // PLANE
        self.y = (self.me // 2) % 2
        self.core = self.me % 2

    def along_z(self, values, step):
        perm = [(d, (d + step * PLANE) % self.size) for d in range(self.size)]
        return lax.ppermute(values, "inner", perm)

    def across_y(self, values):
        return lax.ppermute(values, "inner", [(d, d ^ 2) for d in range(self.size)])

    def across_core(self, values):
        return lax.ppermute(values, "inner", [(d, d ^ 1) for d in range(self.size)])


def add(left, right):
    return (left.astype(jnp.float32) + right.astype(jnp.float32)).astype(jnp.bfloat16)


def after(values, *others):
    return lax.optimization_barrier((values, *others))[0]


def nearest_first(planes):
    return sorted(range(planes), key=lambda k: (min(k, planes - k), k))


def gather_rows(ring, rows):
    chunks = {}
    reached = {}
    for k in nearest_first(ring.planes):
        far = min(k, ring.planes - k)
        if far > 1:
            rows = after(rows, *[reached[j] for j in reached if min(j, ring.planes - j) == far - 1])
        column = ring.along_z(rows, k) if k else rows
        if k:
            reached[k] = column
        crossed = ring.across_y(column)
        if k == 0:
            first = crossed
        half = jnp.concatenate([column, crossed], axis=0)
        chunks[k] = jnp.concatenate([half, ring.across_core(half)], axis=0)
    return chunks, first


def scatter_sum(ring, chunks):
    rows = chunks[0].shape[0] // PLANE
    order = nearest_first(ring.planes)
    total = None
    halves = []
    crossed = []
    for k in order[1:] + order[:1]:
        chunk = chunks[k]
        half = add(chunk[: 2 * rows], ring.across_core(chunk[2 * rows :]))
        away = half[rows:]
        if len(crossed) > 1:
            away = after(away, crossed[-2])
        if k == 0 and halves:
            away = after(away, halves[-1])
        other = ring.across_y(away)
        halves.append(half)
        crossed.append(other)
        part = add(half[:rows], other)
        if k:
            part = ring.along_z(part, -k)
        part = part.astype(jnp.float32)
        total = part if total is None else total + part
    return total


def gate_halves(routes, gates, experts):
    named = routes[:, :, None] == jnp.arange(experts, dtype=jnp.int32)[None, None, :]
    table = jnp.sum(jnp.where(named, gates[:, :, None], 0.0), axis=1)
    high = table.astype(jnp.bfloat16)
    low = (table - high.astype(jnp.float32)).astype(jnp.bfloat16)
    spare = -2 * experts % 128
    return jnp.concatenate([high, low, jnp.zeros((routes.shape[0], spare), jnp.bfloat16)], axis=1)


def gate_column(ring, halves):
    lane = jnp.arange(halves.shape[1], dtype=jnp.int32)[None, :]
    mine = (lane == ring.me) | (lane == ring.me + ring.size)
    return jnp.sum(jnp.where(mine, halves.astype(jnp.float32), 0.0), axis=1, keepdims=True)


def normed(values, gain):
    widened = values.astype(jnp.float32)
    inverse = lax.rsqrt(jnp.mean(widened * widened, axis=-1, keepdims=True) + EPSILON)
    return (widened * inverse * gain).astype(jnp.bfloat16)


def expert(rows, gate_column, gate_up, down):
    width = down.shape[0]
    projected = jnp.dot(rows, gate_up, preferred_element_type=jnp.float32)
    hidden = (jax.nn.silu(projected[:, :width]) * projected[:, width:]).astype(jnp.bfloat16)
    out = jnp.dot(hidden, down, preferred_element_type=jnp.float32)
    return (out * gate_column).astype(jnp.bfloat16)


def experts_on(ring, chunks, width, gate_up, down):
    results = {}
    last = None
    for k in nearest_first(ring.planes):
        chunk = chunks[k] if last is None else after(chunks[k], last)
        last = expert(chunk[:, :width], gate_column(ring, chunk[:, width:]), gate_up, down)
        results[k] = last
    return results


def plane_weight(ring, weight, groups):
    rows = weight.shape[0]
    if groups % 2:
        other = ring.across_y(weight)
    else:
        odd = lax.axis_index("groups") % 2
        sent = lax.dynamic_slice_in_dim(weight, odd * (rows // 2), rows // 2, axis=0)
        here = ring.across_y(sent)
        there = lax.ppermute(here, "groups", [(g, g ^ 1) for g in range(groups)])
        other = jnp.where(odd == 0, jnp.concatenate([here, there]), jnp.concatenate([there, here]))
    pair = jnp.where(ring.y == 0, jnp.concatenate([weight, other]), jnp.concatenate([other, weight]))
    sibling = ring.across_core(pair)
    mine = [pair[:rows], sibling[:rows], pair[rows:], sibling[rows:]]
    theirs = [sibling[:rows], pair[:rows], sibling[rows:], pair[rows:]]
    return jnp.where(ring.core == 0, jnp.concatenate(mine), jnp.concatenate(theirs))


def merge(ring, merged_in, weight):
    rows, features = merged_in.shape
    share = features // ring.planes
    total = None
    for k in reversed(nearest_first(ring.planes)):
        piece = lax.dynamic_slice_in_dim(merged_in, (ring.z + k) % ring.planes * share, share, axis=1)
        if k:
            piece = ring.along_z(piece, k)
        product = jnp.dot(piece, weight, preferred_element_type=jnp.float32)
        if k:
            product = ring.along_z(product.astype(jnp.bfloat16), -k).astype(jnp.float32)
        total = product if total is None else total + product
    return total


def local(
    hidden_rows,
    token_embed,
    first_routes,
    first_gates,
    first_gate_up,
    first_down,
    second_routes,
    second_gates,
    second_gate_up,
    second_down,
    hidden_gain,
    embed_gain,
    merge_weight,
):
    ring = Ring()
    width = hidden_rows.shape[1]
    halves = gate_halves(first_routes, first_gates, ring.size)
    second_halves = gate_halves(second_routes, second_gates, ring.size)
    rows = after(jnp.concatenate([hidden_rows, halves], axis=1), second_halves)
    chunks, crossed = gather_rows(ring, rows)
    weight = plane_weight(ring, after(merge_weight, crossed), lax.axis_size("groups"))
    first = scatter_sum(ring, experts_on(ring, chunks, width, first_gate_up[0], first_down[0]))
    after_first = (hidden_rows.astype(jnp.float32) + first).astype(jnp.bfloat16)
    merged_in = jnp.concatenate([normed(after_first, hidden_gain), normed(token_embed, embed_gain)], axis=1)
    merged = merge(ring, merged_in, weight)
    after_merge = (after_first.astype(jnp.float32) + jax.nn.silu(merged)).astype(jnp.bfloat16)
    chunks, _ = gather_rows(ring, jnp.concatenate([after_merge, second_halves], axis=1))
    second = scatter_sum(ring, experts_on(ring, chunks, width, second_gate_up[0], second_down[0]))
    return (after_merge.astype(jnp.float32) + second).astype(jnp.bfloat16)


def solution(mesh):
    rows = P(("groups", "inner"), None)
    weight = P("inner", None, None)
    return jax.shard_map(
        local,
        mesh=mesh,
        in_specs=(rows, rows, rows, rows, weight, weight, rows, rows, weight, weight, P(), P(), P("inner", None)),
        out_specs=rows,
        check_vma=False,
    )
```

```python
import jax
import jax.numpy as jnp
from jax import lax
from jax.sharding import PartitionSpec as P

EPSILON = 1e-06
PLANES = 4
ORDER = (0, 1, 2, 3)


class Ring:
    def __init__(self):
        self.size = lax.axis_size("inner")
        self.plane = self.size // PLANES
        self.me = lax.axis_index("inner")
        self.z = self.me // self.plane
        self.inside = (self.z == 1) | (self.z == 2)
        self.bits = []
        bit = self.plane // 2
        while bit:
            self.bits.append(bit)
            bit //= 2

    def send(self, values, pairs):
        perm = [(a * self.plane + i, b * self.plane + i) for a, b in pairs for i in range(self.plane)]
        return lax.ppermute(values, "inner", perm)

    def across(self, values, bit):
        return lax.ppermute(values, "inner", [(d, d ^ bit) for d in range(self.size)])

    def high(self, bit):
        return (self.me // bit) % 2 == 1


def after(values, *others):
    return lax.optimization_barrier((values, *others))[0]


def add(*terms):
    return sum(t.astype(jnp.float32) for t in terms).astype(jnp.bfloat16)


def gather_rows(ring, rows, work):
    def fill(column, ties):
        for i, bit in enumerate(ring.bits):
            if i == 1:
                column = after(column, *ties)
            column = jnp.concatenate([column, ring.across(column, bit)], axis=0)
        return column

    done = {}
    slots = {0: rows}
    chunk0 = fill(rows, [])
    slots[1] = ring.send(rows, [(0, 1), (1, 0), (2, 3), (3, 2)])
    middle = ring.send(rows, [(1, 2), (2, 1)])
    chunk1 = fill(slots[1], [])
    near = ring.send(middle, [(1, 0), (2, 3)])
    far = ring.send(slots[1], [(1, 2), (2, 1)])
    slots[2] = jnp.where(ring.inside, far, near)
    done[0] = work(0, chunk0)
    chunk2 = fill(after(slots[2], done[0]), [])
    outer = ring.send(slots[2], [(1, 0), (2, 3)])
    slots[3] = jnp.where(ring.inside, middle, outer)
    done[1] = work(1, after(chunk1, done[0]))
    column3 = after(slots[3], done[1])
    done[2] = work(2, after(chunk2, done[1]))
    chunk3 = fill(column3, [done[2]])
    return done, chunk3


def within_plane(ring, chunk):
    for bit in reversed(ring.bits[1:]):
        rows = chunk.shape[0] // 2
        chunk = add(chunk[:rows], ring.across(chunk[rows:], bit))
    return chunk


def plane_sums(ring, part):
    two = part(2)
    inward = ring.send(two, [(0, 1), (3, 2)])
    swapped = ring.send(two, [(1, 2), (2, 1)])
    three = part(3)
    ends = ring.send(three, [(0, 3), (3, 0)])
    middle = ring.send(add(three, inward), [(1, 2), (2, 1)])
    one = ring.send(add(part(1), swapped), [(0, 1), (1, 0), (2, 3), (3, 2)])
    return sum(t.astype(jnp.float32) for t in (part(0), one, middle, ends))


def gate_halves(layers, experts):
    columns = []
    for routes, gates in layers:
        named = routes[:, :, None] == jnp.arange(experts, dtype=jnp.int32)[None, None, :]
        table = jnp.sum(jnp.where(named, gates[:, :, None], 0.0), axis=1)
        high = table.astype(jnp.bfloat16)
        columns += [high, (table - high.astype(jnp.float32)).astype(jnp.bfloat16)]
    spare = -2 * experts * len(layers) % 128
    return jnp.concatenate(columns + [jnp.zeros((columns[0].shape[0], spare), jnp.bfloat16)], axis=1)


def gate_column(ring, halves, layer):
    lane = jnp.arange(halves.shape[1], dtype=jnp.int32)[None, :]
    first = 2 * layer * ring.size + ring.me
    mine = (lane == first) | (lane == first + ring.size)
    return jnp.sum(jnp.where(mine, halves.astype(jnp.float32), 0.0), axis=1, keepdims=True)


def normed(values, gain):
    widened = values.astype(jnp.float32)
    inverse = lax.rsqrt(jnp.mean(widened * widened, axis=-1, keepdims=True) + EPSILON)
    return (widened * inverse * gain).astype(jnp.bfloat16)


def expert(rows, gates, gate_up, down):
    width = down.shape[0]
    projected = jnp.dot(rows, gate_up, preferred_element_type=jnp.float32)
    hidden = (jax.nn.silu(projected[:, :width]) * projected[:, width:]).astype(jnp.bfloat16)
    out = jnp.dot(hidden, down, preferred_element_type=jnp.float32)
    return (out * gates).astype(jnp.bfloat16)


def routed(ring, rows, work):
    done, chunk3 = gather_rows(ring, rows, work)
    halves = {2: within_plane(ring, done[2])}
    done[3] = work(3, after(chunk3, halves[2]))
    for slot in (3, 1, 0):
        halves[slot] = within_plane(ring, done[slot])
    own = rows.shape[0]
    crossed = {}
    for slot, earlier in ((2, []), (3, []), (1, [2]), (0, [3])):
        away = after(halves[slot][own:], *[crossed[e] for e in earlier], halves[3] if earlier else halves[2])
        crossed[slot] = ring.across(away, ring.bits[0])
    return plane_sums(ring, lambda slot: add(halves[slot][:own], crossed[slot]))


def plane_weight(ring, weight, groups):
    rows = weight.shape[0]
    first = ring.bits[0]
    if groups % 2:
        other = ring.across(weight, first)
    else:
        odd = lax.axis_index("groups") % 2
        sent = lax.dynamic_slice_in_dim(weight, odd * (rows // 2), rows // 2, axis=0)
        here = ring.across(sent, first)
        there = lax.ppermute(here, "groups", [(g, g ^ 1) for g in range(groups)])
        other = jnp.where(odd == 0, jnp.concatenate([here, there]), jnp.concatenate([there, here]))
    held = jnp.where(ring.high(first), jnp.stack([other, weight]), jnp.stack([weight, other]))
    for i, bit in enumerate(ring.bits[1:]):
        other = ring.across(held, bit)
        axis = i + 1
        held = jnp.where(ring.high(bit), jnp.stack([other, held], axis), jnp.stack([held, other], axis))
    return held.reshape(ring.plane * rows, weight.shape[1])


def merge(ring, merged_in, weight):
    share = merged_in.shape[1] // PLANES
    products = {}
    for slot in (2, 3, 1, 0):
        piece = lax.dynamic_slice_in_dim(merged_in, (ring.z ^ slot) * share, share, axis=1)
        if slot:
            piece = ring.send(piece, [(p, p ^ slot) for p in range(PLANES)])
        products[slot] = jnp.dot(piece, weight, preferred_element_type=jnp.float32)
        if slot:
            products[slot] = products[slot].astype(jnp.bfloat16)
    return plane_sums(ring, lambda slot: products[slot])


def local(
    hidden_rows,
    token_embed,
    first_routes,
    first_gates,
    first_gate_up,
    first_down,
    second_routes,
    second_gates,
    second_gate_up,
    second_down,
    hidden_gain,
    embed_gain,
    merge_weight,
):
    ring = Ring()
    width = hidden_rows.shape[1]
    halves = gate_halves([(first_routes, first_gates), (second_routes, second_gates)], ring.size)
    weight = plane_weight(ring, merge_weight, lax.axis_size("groups"))
    second_columns = {}

    def first_work(slot, chunk):
        second_columns[slot] = gate_column(ring, chunk[:, width:], 1)
        gates = gate_column(ring, chunk[:, width:], 0)
        return expert(chunk[:, :width], gates, first_gate_up[0], first_down[0])

    def second_work(slot, chunk):
        return expert(chunk, second_columns[slot], second_gate_up[0], second_down[0])

    first = routed(ring, jnp.concatenate([hidden_rows, halves], axis=1), first_work)
    after_first = (hidden_rows.astype(jnp.float32) + first).astype(jnp.bfloat16)
    merged_in = jnp.concatenate([normed(after_first, hidden_gain), normed(token_embed, embed_gain)], axis=1)
    merged = merge(ring, merged_in, weight)
    after_merge = (after_first.astype(jnp.float32) + jax.nn.silu(merged)).astype(jnp.bfloat16)
    second = routed(ring, after_merge, second_work)
    return (after_merge.astype(jnp.float32) + second).astype(jnp.bfloat16)


def solution(mesh):
    rows = P(("groups", "inner"), None)
    weight = P("inner", None, None)
    return jax.shard_map(
        local,
        mesh=mesh,
        in_specs=(rows, rows, rows, rows, weight, weight, rows, rows, weight, weight, P(), P(), P("inner", None)),
        out_specs=rows,
        check_vma=False,
    )
```

```python
import jax
import jax.numpy as jnp
from jax import lax
from jax.sharding import PartitionSpec as P

EPSILON = 1e-06
PLANES = 4
PARTS = 2


class Ring:
    def __init__(self):
        self.size = lax.axis_size("inner")
        self.plane = self.size // PLANES
        self.me = lax.axis_index("inner")
        self.z = self.me // self.plane
        self.inside = (self.z == 1) | (self.z == 2)
        self.bits = []
        bit = self.plane // 2
        while bit:
            self.bits.append(bit)
            bit //= 2

    def send(self, values, pairs):
        perm = [(a * self.plane + i, b * self.plane + i) for a, b in pairs for i in range(self.plane)]
        return lax.ppermute(values, "inner", perm)

    def across(self, values, bit):
        return lax.ppermute(values, "inner", [(d, d ^ bit) for d in range(self.size)])

    def same_core(self):
        return [list(range(c, self.size, 2)) for c in range(2)]

    def high(self, bit):
        return (self.me // bit) % 2 == 1


def after(values, *others):
    return lax.optimization_barrier((values, *others))[0]


def add(*terms):
    return sum(t.astype(jnp.float32) for t in terms).astype(jnp.bfloat16)


def plane_sums(ring, part):
    two = part(2)
    inward = ring.send(two, [(0, 1), (3, 2)])
    swapped = ring.send(two, [(1, 2), (2, 1)])
    three = part(3)
    ends = ring.send(three, [(0, 3), (3, 0)])
    middle = ring.send(add(three, inward), [(1, 2), (2, 1)])
    one = ring.send(add(part(1), swapped), [(0, 1), (1, 0), (2, 3), (3, 2)])
    return sum(t.astype(jnp.float32) for t in (part(0), one, middle, ends))


def gate_halves(layers, experts):
    columns = []
    for routes, gates in layers:
        named = routes[:, :, None] == jnp.arange(experts, dtype=jnp.int32)[None, None, :]
        table = jnp.sum(jnp.where(named, gates[:, :, None], 0.0), axis=1)
        high = table.astype(jnp.bfloat16)
        columns += [high, (table - high.astype(jnp.float32)).astype(jnp.bfloat16)]
    spare = -2 * experts * len(layers) % 128
    return jnp.concatenate(columns + [jnp.zeros((columns[0].shape[0], spare), jnp.bfloat16)], axis=1)


def gate_column(ring, halves, layer):
    lane = jnp.arange(halves.shape[1], dtype=jnp.int32)[None, :]
    first = 2 * layer * ring.size + ring.me
    mine = (lane == first) | (lane == first + ring.size)
    return jnp.sum(jnp.where(mine, halves.astype(jnp.float32), 0.0), axis=1, keepdims=True)


def normed(values, gain):
    widened = values.astype(jnp.float32)
    inverse = lax.rsqrt(jnp.mean(widened * widened, axis=-1, keepdims=True) + EPSILON)
    return (widened * inverse * gain).astype(jnp.bfloat16)


def expert(rows, gates, gate_up, down):
    width = down.shape[0]
    projected = jnp.dot(rows, gate_up, preferred_element_type=jnp.float32)
    hidden = (jax.nn.silu(projected[:, :width]) * projected[:, width:]).astype(jnp.bfloat16)
    out = jnp.dot(hidden, down, preferred_element_type=jnp.float32)
    return (out * gates).astype(jnp.bfloat16)


def routed(ring, rows, work):
    count = rows.shape[0] // PARTS
    sums = []
    for part in range(PARTS):
        mine = lax.all_gather(
            rows[part * count : (part + 1) * count], "inner", axis_index_groups=ring.same_core(), axis=0, tiled=True
        )
        every = jnp.concatenate([mine, ring.across(mine, 1)], axis=0)
        out = work(part, every)
        half = out.shape[0] // 2
        pair = add(out[:half], ring.across(out[half:], 1))
        sums.append(
            lax.psum_scatter(pair, "inner", axis_index_groups=ring.same_core(), scatter_dimension=0, tiled=True)
        )
    return jnp.concatenate(sums, axis=0).astype(jnp.float32)


def plane_weight(ring, weight, groups):
    rows = weight.shape[0]
    first = ring.bits[0]
    if groups % 2:
        other = ring.across(weight, first)
    else:
        odd = lax.axis_index("groups") % 2
        sent = lax.dynamic_slice_in_dim(weight, odd * (rows // 2), rows // 2, axis=0)
        here = ring.across(sent, first)
        there = lax.ppermute(here, "groups", [(g, g ^ 1) for g in range(groups)])
        other = jnp.where(odd == 0, jnp.concatenate([here, there]), jnp.concatenate([there, here]))
    held = jnp.where(ring.high(first), jnp.stack([other, weight]), jnp.stack([weight, other]))
    for i, bit in enumerate(ring.bits[1:]):
        other = ring.across(held, bit)
        axis = i + 1
        held = jnp.where(ring.high(bit), jnp.stack([other, held], axis), jnp.stack([held, other], axis))
    return held.reshape(ring.plane * rows, weight.shape[1])


def merge(ring, merged_in, weight):
    share = merged_in.shape[1] // PLANES
    products = {}
    for slot in (2, 3, 1, 0):
        piece = lax.dynamic_slice_in_dim(merged_in, (ring.z ^ slot) * share, share, axis=1)
        if slot:
            piece = ring.send(piece, [(p, p ^ slot) for p in range(PLANES)])
        products[slot] = jnp.dot(piece, weight, preferred_element_type=jnp.float32)
        if slot:
            products[slot] = products[slot].astype(jnp.bfloat16)
    return plane_sums(ring, lambda slot: products[slot])


def local(
    hidden_rows,
    token_embed,
    first_routes,
    first_gates,
    first_gate_up,
    first_down,
    second_routes,
    second_gates,
    second_gate_up,
    second_down,
    hidden_gain,
    embed_gain,
    merge_weight,
):
    ring = Ring()
    width = hidden_rows.shape[1]
    halves = gate_halves([(first_routes, first_gates), (second_routes, second_gates)], ring.size)
    weight = plane_weight(ring, merge_weight, lax.axis_size("groups"))
    second_columns = {}

    def first_work(part, chunk):
        second_columns[part] = gate_column(ring, chunk[:, width:], 1)
        gates = gate_column(ring, chunk[:, width:], 0)
        return expert(chunk[:, :width], gates, first_gate_up[0], first_down[0])

    def second_work(part, chunk):
        return expert(chunk, second_columns[part], second_gate_up[0], second_down[0])

    first = routed(ring, jnp.concatenate([hidden_rows, halves], axis=1), first_work)
    after_first = (hidden_rows.astype(jnp.float32) + first).astype(jnp.bfloat16)
    merged_in = jnp.concatenate([normed(after_first, hidden_gain), normed(token_embed, embed_gain)], axis=1)
    merged = merge(ring, merged_in, weight)
    after_merge = (after_first.astype(jnp.float32) + jax.nn.silu(merged)).astype(jnp.bfloat16)
    second = routed(ring, after_merge, second_work)
    return (after_merge.astype(jnp.float32) + second).astype(jnp.bfloat16)


def solution(mesh):
    rows = P(("groups", "inner"), None)
    weight = P("inner", None, None)
    return jax.shard_map(
        local,
        mesh=mesh,
        in_specs=(rows, rows, rows, rows, weight, weight, rows, rows, weight, weight, P(), P(), P("inner", None)),
        out_specs=rows,
        check_vma=False,
    )
```

```python
import jax
import jax.numpy as jnp
from jax import lax
from jax.sharding import PartitionSpec as P

EPSILON = 1e-06
PLANES = 4
PARTS = 2


class Ring:
    def __init__(self):
        self.size = lax.axis_size("inner")
        self.plane = self.size // PLANES
        self.me = lax.axis_index("inner")
        self.z = self.me // self.plane
        self.bits = []
        bit = self.plane // 2
        while bit:
            self.bits.append(bit)
            bit //= 2

    def between(self, values, slot):
        step = slot * self.plane
        return lax.ppermute(values, "inner", [(d, d ^ step) for d in range(self.size)]) if slot else values

    def across(self, values, bit):
        return lax.ppermute(values, "inner", [(d, d ^ bit) for d in range(self.size)])

    def high(self, bit):
        return (self.me // bit) % 2 == 1


def add(*terms):
    return sum(t.astype(jnp.float32) for t in terms).astype(jnp.bfloat16)


def gather_rows(ring, rows):
    rows = jnp.concatenate([ring.between(rows, slot) for slot in range(PLANES)], axis=0)
    for bit in ring.bits:
        rows = jnp.concatenate([rows, ring.across(rows, bit)], axis=0)
    return rows


def plane_sums(ring, parts):
    return sum(ring.between(part, slot).astype(jnp.float32) for slot, part in enumerate(parts))


def scatter_sum(ring, rows):
    for bit in reversed(ring.bits):
        half = rows.shape[0] // 2
        rows = add(rows[:half], ring.across(rows[half:], bit))
    return plane_sums(ring, jnp.split(rows, PLANES))


def gate_lanes(layers):
    lanes = []
    for routes, gates in layers:
        high = gates.astype(jnp.bfloat16)
        lanes += [routes.astype(jnp.bfloat16), high, (gates - high.astype(jnp.float32)).astype(jnp.bfloat16)]
    lanes = jnp.concatenate(lanes, axis=1)
    return jnp.pad(lanes, ((0, 0), (0, -lanes.shape[1] % 128)))


def gate_column(ring, lanes, layer, top):
    named, high, low = (lanes[:, (3 * layer + i) * top :][:, :top].astype(jnp.float32) for i in range(3))
    return jnp.sum(jnp.where(named == ring.me.astype(jnp.float32), high + low, 0.0), axis=1, keepdims=True)


def normed(values, gain):
    widened = values.astype(jnp.float32)
    inverse = lax.rsqrt(jnp.mean(widened * widened, axis=-1, keepdims=True) + EPSILON)
    return (widened * inverse * gain).astype(jnp.bfloat16)


def expert(rows, gates, gate_up, down):
    width = down.shape[0]
    projected = jnp.dot(rows, gate_up, preferred_element_type=jnp.float32)
    hidden = (jax.nn.silu(projected[:, :width]) * projected[:, width:]).astype(jnp.bfloat16)
    out = jnp.dot(hidden, down, preferred_element_type=jnp.float32)
    return (out * gates).astype(jnp.bfloat16)


def plane_weight(ring, weight, groups):
    rows = weight.shape[0]
    first = ring.bits[0]
    if groups % 2:
        other = ring.across(weight, first)
    else:
        odd = lax.axis_index("groups") % 2
        sent = lax.dynamic_slice_in_dim(weight, odd * (rows // 2), rows // 2, axis=0)
        here = ring.across(sent, first)
        there = lax.ppermute(here, "groups", [(g, g ^ 1) for g in range(groups)])
        other = jnp.where(odd == 0, jnp.concatenate([here, there]), jnp.concatenate([there, here]))
    held = jnp.where(ring.high(first), jnp.stack([other, weight]), jnp.stack([weight, other]))
    for i, bit in enumerate(ring.bits[1:]):
        other = ring.across(held, bit)
        axis = i + 1
        held = jnp.where(ring.high(bit), jnp.stack([other, held], axis), jnp.stack([held, other], axis))
    return held.reshape(ring.plane * rows, weight.shape[1])


def merge(ring, merged_in, weight):
    share = merged_in.shape[1] // PLANES
    pieces = []
    for slot in range(PLANES):
        piece = lax.dynamic_slice_in_dim(merged_in, (ring.z ^ slot) * share, share, axis=1)
        pieces.append(ring.between(piece, slot))
    products = jnp.dot(jnp.concatenate(pieces, axis=0), weight, preferred_element_type=jnp.float32)
    return plane_sums(ring, jnp.split(products.astype(jnp.bfloat16), PLANES))


def local(
    hidden_rows,
    token_embed,
    first_routes,
    first_gates,
    first_gate_up,
    first_down,
    second_routes,
    second_gates,
    second_gate_up,
    second_down,
    hidden_gain,
    embed_gain,
    merge_weight,
):
    ring = Ring()
    width = hidden_rows.shape[1]
    top = first_routes.shape[1]
    lanes = gate_lanes([(first_routes, first_gates), (second_routes, second_gates)])
    weight = plane_weight(ring, merge_weight, lax.axis_size("groups"))

    def program(hidden, embed, lanes):
        chunk = gather_rows(ring, jnp.concatenate([hidden, lanes], axis=1))
        gates = [gate_column(ring, chunk[:, width:], layer, top) for layer in range(2)]
        first = scatter_sum(ring, expert(chunk[:, :width], gates[0], first_gate_up[0], first_down[0]))
        after_first = (hidden.astype(jnp.float32) + first).astype(jnp.bfloat16)
        merged_in = jnp.concatenate([normed(after_first, hidden_gain), normed(embed, embed_gain)], axis=1)
        merged = merge(ring, merged_in, weight)
        after_merge = (after_first.astype(jnp.float32) + jax.nn.silu(merged)).astype(jnp.bfloat16)
        chunk = gather_rows(ring, after_merge)
        second = scatter_sum(ring, expert(chunk, gates[1], second_gate_up[0], second_down[0]))
        return (after_merge.astype(jnp.float32) + second).astype(jnp.bfloat16)

    count = hidden_rows.shape[0] // PARTS
    parts = [slice(p * count, (p + 1) * count) for p in range(PARTS)]
    return jnp.concatenate([program(hidden_rows[p], token_embed[p], lanes[p]) for p in parts], axis=0)


def solution(mesh):
    rows = P(("groups", "inner"), None)
    weight = P("inner", None, None)
    return jax.shard_map(
        local,
        mesh=mesh,
        in_specs=(rows, rows, rows, rows, weight, weight, rows, rows, weight, weight, P(), P(), P("inner", None)),
        out_specs=rows,
        check_vma=False,
    )
```

```python
import jax
import jax.numpy as jnp
from jax import lax
from jax.sharding import PartitionSpec as P

EPSILON = 1e-06
PLANES = 4


class Ring:
    def __init__(self):
        self.size = lax.axis_size("inner")
        self.plane = self.size // PLANES
        self.me = lax.axis_index("inner")
        self.z = self.me // self.plane
        self.inside = (self.z == 1) | (self.z == 2)
        self.bits = []
        bit = self.plane // 2
        while bit:
            self.bits.append(bit)
            bit //= 2

    def send(self, values, pairs):
        perm = [(a * self.plane + i, b * self.plane + i) for a, b in pairs for i in range(self.plane)]
        return lax.ppermute(values, "inner", perm)

    def between(self, values, slot):
        return self.send(values, [(p, p ^ slot) for p in range(PLANES)]) if slot else values

    def across(self, values, bit):
        return lax.ppermute(values, "inner", [(d, d ^ bit) for d in range(self.size)])

    def high(self, bit):
        return (self.me // bit) % 2 == 1


def after(values, *others):
    return lax.optimization_barrier((values, *others))[0]


def add(*terms):
    return sum(t.astype(jnp.float32) for t in terms).astype(jnp.bfloat16)


def within_plane(ring, chunk):
    for bit in reversed(ring.bits[1:]):
        rows = chunk.shape[0] // 2
        chunk = add(chunk[:rows], ring.across(chunk[rows:], bit))
    return chunk


def plane_sums(ring, part):
    return sum(ring.between(part(slot), slot).astype(jnp.float32) for slot in (0, 3, 2, 1))


def gate_lanes(layers):
    lanes = []
    for routes, gates in layers:
        high = gates.astype(jnp.bfloat16)
        lanes += [routes.astype(jnp.bfloat16), high, (gates - high.astype(jnp.float32)).astype(jnp.bfloat16)]
    lanes = jnp.concatenate(lanes, axis=1)
    return jnp.pad(lanes, ((0, 0), (0, -lanes.shape[1] % 128)))


def gate_column(ring, lanes, layer, top):
    named, high, low = (lanes[:, (3 * layer + i) * top :][:, :top].astype(jnp.float32) for i in range(3))
    return jnp.sum(jnp.where(named == ring.me.astype(jnp.float32), high + low, 0.0), axis=1, keepdims=True)


def normed(values, gain):
    widened = values.astype(jnp.float32)
    inverse = lax.rsqrt(jnp.mean(widened * widened, axis=-1, keepdims=True) + EPSILON)
    return (widened * inverse * gain).astype(jnp.bfloat16)


def expert(rows, gates, gate_up, down):
    width = down.shape[0]
    projected = jnp.dot(rows, gate_up, preferred_element_type=jnp.float32)
    hidden = (jax.nn.silu(projected[:, :width]) * projected[:, width:]).astype(jnp.bfloat16)
    out = jnp.dot(hidden, down, preferred_element_type=jnp.float32)
    return (out * gates).astype(jnp.bfloat16)


def routed(ring, rows, work):
    top = ring.bits[0]
    columns = {0: rows, 1: ring.between(rows, 1)}
    crossed = {0: ring.across(rows, top)}
    middle = ring.send(rows, [(1, 2), (2, 1)])
    ends = ring.send(rows, [(0, 3), (3, 0)])
    near = ring.send(middle, [(1, 0), (2, 3)])
    far = ring.send(columns[1], [(1, 2), (2, 1)])
    columns[3] = jnp.where(ring.inside, middle, ends)
    columns[2] = jnp.where(ring.inside, far, near)
    crossed[1] = ring.across(after(columns[1], middle), top)
    crossed[3] = ring.across(columns[3], top)
    crossed[2] = ring.across(columns[2], top)

    done = {}
    halves = {}
    last = [columns[2], crossed[1], crossed[3]]
    for slot in (0, 1, 3, 2):
        chunk = jnp.concatenate([columns[slot], crossed[slot]], axis=0)
        if slot == 2:
            chunk = after(chunk, *last)
            halves[3] = within_plane(ring, done[3])
            last = [halves[3]]
        for bit in ring.bits[1:]:
            chunk = jnp.concatenate([chunk, ring.across(chunk, bit)], axis=0)
        done[slot] = work(slot, after(chunk, *last))
        last = [done[slot]]
    for slot in (2, 1, 0):
        halves[slot] = within_plane(ring, done[slot])

    own = rows.shape[0]
    back = {}
    for slot, ties in ((3, []), (2, []), (1, [3]), (0, [2])):
        away = after(halves[slot][own:], *[back[t] for t in ties], *([halves[2]] if ties else []))
        back[slot] = ring.across(away, top)
    sums = plane_sums(ring, lambda slot: add(halves[slot][:own], back[slot]))
    return sums, [crossed[1], crossed[2], back[2]]


def other_half(ring, weight, groups, ties):
    top = ring.bits[0]
    rows = weight.shape[0] // 2
    odd = lax.axis_index("groups") % 2
    pieces = []
    for piece, (begin, swap) in enumerate(ties):
        if groups % 2:
            pieces.append(ring.across(after(weight[piece * rows : (piece + 1) * rows], *begin), top))
            continue
        sent = lax.dynamic_slice_in_dim(weight, piece * rows + odd * (rows // 2), rows // 2, axis=0)
        here = after(ring.across(after(sent, *begin), top), *swap)
        there = lax.ppermute(here, "groups", [(g, g ^ 1) for g in range(groups)])
        pieces += [jnp.where(odd == 0, here, there), jnp.where(odd == 0, there, here)]
    return jnp.concatenate(pieces, axis=0)


def plane_weight(ring, weight, other):
    held = jnp.where(ring.high(ring.bits[0]), jnp.stack([other, weight]), jnp.stack([weight, other]))
    for i, bit in enumerate(ring.bits[1:]):
        other = ring.across(held, bit)
        axis = i + 1
        held = jnp.where(ring.high(bit), jnp.stack([other, held], axis), jnp.stack([held, other], axis))
    return held.reshape(ring.plane * weight.shape[0], weight.shape[1])


def merge(ring, merged_in, weight):
    share = merged_in.shape[1] // PLANES
    products = {}
    for slot in (2, 3, 1, 0):
        piece = lax.dynamic_slice_in_dim(merged_in, (ring.z ^ slot) * share, share, axis=1)
        products[slot] = jnp.dot(ring.between(piece, slot), weight, preferred_element_type=jnp.float32)
        if slot:
            products[slot] = products[slot].astype(jnp.bfloat16)
    return plane_sums(ring, lambda slot: products[slot])


def local(
    hidden_rows,
    token_embed,
    first_routes,
    first_gates,
    first_gate_up,
    first_down,
    second_routes,
    second_gates,
    second_gate_up,
    second_down,
    hidden_gain,
    embed_gain,
    merge_weight,
):
    ring = Ring()
    width = hidden_rows.shape[1]
    lanes = gate_lanes([(first_routes, first_gates), (second_routes, second_gates)])
    top = first_routes.shape[1]
    second_columns = {}

    def first_work(slot, chunk):
        second_columns[slot] = gate_column(ring, chunk[:, width:], 1, top)
        gates = gate_column(ring, chunk[:, width:], 0, top)
        return expert(chunk[:, :width], gates, first_gate_up[0], first_down[0])

    def second_work(slot, chunk):
        return expert(chunk, second_columns[slot], second_gate_up[0], second_down[0])

    first, steps = routed(ring, jnp.concatenate([hidden_rows, lanes], axis=1), first_work)
    ties = [([], [steps[0]]), ([steps[1]], [steps[2]])]
    weight = plane_weight(ring, merge_weight, other_half(ring, merge_weight, lax.axis_size("groups"), ties))
    after_first = (hidden_rows.astype(jnp.float32) + first).astype(jnp.bfloat16)
    merged_in = jnp.concatenate([normed(after_first, hidden_gain), normed(token_embed, embed_gain)], axis=1)
    merged = merge(ring, merged_in, weight)
    after_merge = (after_first.astype(jnp.float32) + jax.nn.silu(merged)).astype(jnp.bfloat16)
    second, _ = routed(ring, after_merge, second_work)
    return (after_merge.astype(jnp.float32) + second).astype(jnp.bfloat16)


def solution(mesh):
    rows = P(("groups", "inner"), None)
    weight = P("inner", None, None)
    return jax.shard_map(
        local,
        mesh=mesh,
        in_specs=(rows, rows, rows, rows, weight, weight, rows, rows, weight, weight, P(), P(), P("inner", None)),
        out_specs=rows,
        check_vma=False,
    )
```

```python
import jax
import jax.numpy as jnp
from jax import lax
from jax.sharding import PartitionSpec as P

EPSILON = 1e-06
PLANES = 4


class Ring:
    def __init__(self):
        self.size = lax.axis_size("inner")
        self.plane = self.size // PLANES
        self.me = lax.axis_index("inner")
        self.z = self.me // self.plane
        self.inside = (self.z == 1) | (self.z == 2)
        self.bits = []
        bit = self.plane // 2
        while bit:
            self.bits.append(bit)
            bit //= 2

    def send(self, values, pairs):
        perm = [(a * self.plane + i, b * self.plane + i) for a, b in pairs for i in range(self.plane)]
        return lax.ppermute(values, "inner", perm)

    def between(self, values, slot):
        return self.send(values, [(p, p ^ slot) for p in range(PLANES)]) if slot else values

    def across(self, values, bit):
        return lax.ppermute(values, "inner", [(d, d ^ bit) for d in range(self.size)])

    def high(self, bit):
        return (self.me // bit) % 2 == 1


def after(values, *others):
    return lax.optimization_barrier((values, *others))[0]


def add(*terms):
    return sum(t.astype(jnp.float32) for t in terms).astype(jnp.bfloat16)


def within_plane(ring, chunk):
    for bit in reversed(ring.bits[1:]):
        rows = chunk.shape[0] // 2
        chunk = add(chunk[:rows], ring.across(chunk[rows:], bit))
    return chunk


def plane_sums(ring, part):
    return sum(ring.between(part(slot), slot).astype(jnp.float32) for slot in (0, 3, 2, 1))


def gate_lanes(layers):
    pieces = []
    for routes, gates in layers:
        high = gates.astype(jnp.bfloat16).astype(jnp.float32)
        pieces += [routes.astype(jnp.float32), high, gates - high]
    top = pieces[0].shape[1]
    width = -(-top * len(pieces) // 128) * 128
    placed = [jnp.pad(p, ((0, 0), (i * top, width - (i + 1) * top))) for i, p in enumerate(pieces)]
    return sum(placed).astype(jnp.bfloat16)


def gate_column(ring, lanes, layer, top):
    named, high, low = (lanes[:, (3 * layer + i) * top :][:, :top].astype(jnp.float32) for i in range(3))
    return jnp.sum(jnp.where(named == ring.me.astype(jnp.float32), high + low, 0.0), axis=1, keepdims=True)


def normed(values, gain):
    widened = values.astype(jnp.float32)
    inverse = lax.rsqrt(jnp.mean(widened * widened, axis=-1, keepdims=True) + EPSILON)
    return (widened * inverse * gain).astype(jnp.bfloat16)


def expert(rows, gates, gate_up, down):
    width = down.shape[0]
    projected = jnp.dot(rows, gate_up, preferred_element_type=jnp.float32)
    hidden = (jax.nn.silu(projected[:, :width]) * projected[:, width:]).astype(jnp.bfloat16)
    out = jnp.dot(hidden, down, preferred_element_type=jnp.float32)
    return (out * gates).astype(jnp.bfloat16)


def routed(ring, rows, work):
    top = ring.bits[0]
    columns = {0: rows, 1: ring.between(rows, 1)}
    crossed = {0: ring.across(rows, top)}
    middle = ring.send(rows, [(1, 2), (2, 1)])
    ends = ring.send(rows, [(0, 3), (3, 0)])
    near = ring.send(middle, [(1, 0), (2, 3)])
    far = ring.send(columns[1], [(1, 2), (2, 1)])
    columns[3] = jnp.where(ring.inside, middle, ends)
    columns[2] = jnp.where(ring.inside, far, near)
    crossed[1] = ring.across(after(columns[1], crossed[0]), top)
    crossed[3] = ring.across(after(columns[3], crossed[0]), top)
    crossed[2] = ring.across(after(columns[2], crossed[1]), top)

    chunks = {}
    for slot in (3, 0, 1, 2):
        chunks[slot] = jnp.concatenate([columns[slot], crossed[slot]], axis=0)
        for bit in ring.bits[1:]:
            chunks[slot] = jnp.concatenate([chunks[slot], ring.across(chunks[slot], bit)], axis=0)

    own = rows.shape[0]
    halves = {}
    back = {}

    def turn(slot, *ties):
        done = work(slot, after(chunks[slot], *ties))
        halves[slot] = within_plane(ring, done)
        return done

    turn(3, columns[2], crossed[1], crossed[3])
    back[3] = ring.across(halves[3][own:], top)
    second = turn(1, turn(0, halves[3]))
    turn(2, second, back[3])
    back[2] = ring.across(halves[2][own:], top)
    back[1] = ring.across(after(halves[1][own:], halves[2]), top)
    back[0] = ring.across(after(halves[0][own:], halves[2], back[2]), top)
    sums = plane_sums(ring, lambda slot: add(halves[slot][:own], back[slot]))
    return sums, columns[2]


def shared_weight(ring, weight):
    other = ring.between(weight, 1)
    held = jnp.where(ring.z % 2 == 1, jnp.stack([other, weight]), jnp.stack([weight, other]))
    for i, bit in enumerate(ring.bits[1:]):
        other = ring.across(held, bit)
        axis = i + 1
        held = jnp.where(ring.high(bit), jnp.stack([other, held], axis), jnp.stack([held, other], axis))
    return held.reshape(ring.plane * weight.shape[0], weight.shape[1])


def merge(ring, merged_in, weight):
    top = ring.bits[0]
    share = merged_in.shape[1] // (2 * PLANES)
    steps = ((1, 1), (1, 0), (0, 1), (0, 0))
    pieces = []
    for far, side in steps:
        start = (2 * (ring.z // 2 ^ far) * 2 + (ring.high(top).astype(jnp.int32) ^ side)) * share
        halves = [lax.dynamic_slice_in_dim(merged_in, start + low * 2 * share, share, axis=1) for low in range(2)]
        piece = jnp.concatenate(halves, axis=1)
        crossing = far * 2 * ring.plane + side * top
        pieces.append(ring.across(piece, crossing) if crossing else piece)
    pieces[0] = after(pieces[0], *pieces[1:3])
    products = {s: jnp.dot(p, weight, preferred_element_type=jnp.float32) for s, p in zip(steps, pieces)}
    beyond = ring.across(products[1, 1].astype(jnp.bfloat16), top)
    beside = ring.across(products[0, 1].astype(jnp.bfloat16), top)
    away = ring.between(add(products[1, 0], beyond), 2)
    return products[0, 0] + beside.astype(jnp.float32) + away.astype(jnp.float32)


def local(
    hidden_rows,
    token_embed,
    first_routes,
    first_gates,
    first_gate_up,
    first_down,
    second_routes,
    second_gates,
    second_gate_up,
    second_down,
    hidden_gain,
    embed_gain,
    merge_weight,
):
    ring = Ring()
    width = hidden_rows.shape[1]
    lanes = gate_lanes([(first_routes, first_gates), (second_routes, second_gates)])
    top = first_routes.shape[1]
    second_columns = {}

    def first_work(slot, chunk):
        second_columns[slot] = gate_column(ring, chunk[:, width:], 1, top)
        gates = gate_column(ring, chunk[:, width:], 0, top)
        return expert(chunk[:, :width], gates, first_gate_up[0], first_down[0])

    def second_work(slot, chunk):
        return expert(chunk, second_columns[slot], second_gate_up[0], second_down[0])

    first, gathered = routed(ring, jnp.concatenate([hidden_rows, lanes], axis=1), first_work)
    weight = shared_weight(ring, after(merge_weight, gathered))
    after_first = (hidden_rows.astype(jnp.float32) + first).astype(jnp.bfloat16)
    merged_in = jnp.concatenate([normed(after_first, hidden_gain), normed(token_embed, embed_gain)], axis=1)
    merged = merge(ring, merged_in, weight)
    after_merge = (after_first.astype(jnp.float32) + jax.nn.silu(merged)).astype(jnp.bfloat16)
    second, _ = routed(ring, after_merge, second_work)
    return (after_merge.astype(jnp.float32) + second).astype(jnp.bfloat16)


def solution(mesh):
    rows = P(("groups", "inner"), None)
    weight = P("inner", None, None)
    return jax.shard_map(
        local,
        mesh=mesh,
        in_specs=(rows, rows, rows, rows, weight, weight, rows, rows, weight, weight, P(), P(), P("inner", None)),
        out_specs=rows,
        check_vma=False,
    )
```

```python
import jax
import jax.numpy as jnp
from jax import lax
from jax.sharding import PartitionSpec as P

EPSILON = 1e-06
PLANES = 4


class Ring:
    def __init__(self):
        self.size = lax.axis_size("inner")
        self.plane = self.size // PLANES
        self.me = lax.axis_index("inner")
        self.z = self.me // self.plane
        self.inside = (self.z == 1) | (self.z == 2)
        self.bits = []
        bit = self.plane // 2
        while bit:
            self.bits.append(bit)
            bit //= 2

    def send(self, values, pairs):
        perm = [(a * self.plane + i, b * self.plane + i) for a, b in pairs for i in range(self.plane)]
        return lax.ppermute(values, "inner", perm)

    def between(self, values, slot):
        return self.send(values, [(p, p ^ slot) for p in range(PLANES)]) if slot else values

    def across(self, values, bit):
        return lax.ppermute(values, "inner", [(d, d ^ bit) for d in range(self.size)])

    def high(self, bit):
        return (self.me // bit) % 2 == 1


def after(values, *others):
    return lax.optimization_barrier((values, *others))[0]


def add(*terms):
    return sum(t.astype(jnp.float32) for t in terms).astype(jnp.bfloat16)


def within_plane(ring, chunk):
    for bit in reversed(ring.bits[1:]):
        rows = chunk.shape[0] // 2
        chunk = add(chunk[:rows], ring.across(chunk[rows:], bit))
    return chunk


def plane_sums(ring, part):
    return sum(ring.between(part(slot), slot).astype(jnp.float32) for slot in (0, 3, 2, 1))


def gate_lanes(layers):
    pieces = []
    for routes, gates in layers:
        high = gates.astype(jnp.bfloat16).astype(jnp.float32)
        pieces += [routes.astype(jnp.float32), high, gates - high]
    top = pieces[0].shape[1]
    width = -(-top * len(pieces) // 128) * 128
    placed = [jnp.pad(p, ((0, 0), (i * top, width - (i + 1) * top))) for i, p in enumerate(pieces)]
    return sum(placed).astype(jnp.bfloat16)


def gate_column(ring, lanes, layer, top):
    named, high, low = (lanes[:, (3 * layer + i) * top :][:, :top].astype(jnp.float32) for i in range(3))
    return jnp.sum(jnp.where(named == ring.me.astype(jnp.float32), high + low, 0.0), axis=1, keepdims=True)


def normed(values, gain):
    widened = values.astype(jnp.float32)
    inverse = lax.rsqrt(jnp.mean(widened * widened, axis=-1, keepdims=True) + EPSILON)
    return (widened * inverse * gain).astype(jnp.bfloat16)


def expert(rows, gates, gate_up, down):
    width = down.shape[0]
    projected = jnp.dot(rows, gate_up, preferred_element_type=jnp.float32)
    hidden = (jax.nn.silu(projected[:, :width]) * projected[:, width:]).astype(jnp.bfloat16)
    out = jnp.dot(hidden, down, preferred_element_type=jnp.float32)
    return (out * gates).astype(jnp.bfloat16)


def routed(ring, rows, work):
    top = ring.bits[0]
    columns = {0: rows, 1: ring.between(rows, 1)}
    crossed = {0: ring.across(rows, top)}
    middle = ring.send(rows, [(1, 2), (2, 1)])
    ends = ring.send(rows, [(0, 3), (3, 0)])
    near = ring.send(middle, [(1, 0), (2, 3)])
    far = ring.send(columns[1], [(1, 2), (2, 1)])
    columns[3] = jnp.where(ring.inside, middle, ends)
    columns[2] = jnp.where(ring.inside, far, near)
    crossed[1] = ring.across(after(columns[1], middle), top)
    crossed[3] = ring.across(columns[3], top)
    crossed[2] = ring.across(columns[2], top)

    def chunk(slot, *ties):
        values = after(jnp.concatenate([columns[slot], crossed[slot]], axis=0), *ties)
        for bit in ring.bits[1:]:
            values = jnp.concatenate([values, ring.across(values, bit)], axis=0)
        return values

    own = rows.shape[0]
    halves = {}
    back = {}

    def turn(slot, rows, *ties):
        done = work(slot, after(rows, *ties))
        halves[slot] = within_plane(ring, done)
        return done

    def swap(slot, *ties):
        back[slot] = ring.across(after(halves[slot][own:], *ties), top)
        parts[slot] = add(halves[slot][:own], back[slot])

    parts = {}
    last = [columns[2], crossed[1], crossed[3]]
    for slot in (3, 0, 1):
        last = [turn(slot, chunk(slot), *last)]
    turn(2, chunk(2, *last), halves[3])
    swap(3)
    swap(2)
    swap(1, halves[2], back[3])
    swap(0, halves[2], back[2])
    sums = plane_sums(ring, lambda slot: parts[slot])
    return sums, columns[2], back[0]


def shared_weight(ring, weight, *ties):
    other = after(ring.between(weight, 1), *ties)
    held = jnp.where(ring.z % 2 == 1, jnp.stack([other, weight]), jnp.stack([weight, other]))
    for i, bit in enumerate(ring.bits[1:]):
        other = ring.across(held, bit)
        axis = i + 1
        held = jnp.where(ring.high(bit), jnp.stack([other, held], axis), jnp.stack([held, other], axis))
    return held.reshape(ring.plane * weight.shape[0], weight.shape[1])


def merge(ring, merged_in, weight):
    top = ring.bits[0]
    share = merged_in.shape[1] // (2 * PLANES)
    steps = ((1, 1), (1, 0), (0, 1), (0, 0))
    pieces = []
    for far, side in steps:
        start = (2 * (ring.z // 2 ^ far) * 2 + (ring.high(top).astype(jnp.int32) ^ side)) * share
        halves = [lax.dynamic_slice_in_dim(merged_in, start + low * 2 * share, share, axis=1) for low in range(2)]
        piece = jnp.concatenate(halves, axis=1)
        crossing = far * 2 * ring.plane + side * top
        pieces.append(ring.across(piece, crossing) if crossing else piece)
    pieces[0] = after(pieces[0], *pieces[1:3])
    products = {s: jnp.dot(p, weight, preferred_element_type=jnp.float32) for s, p in zip(steps, pieces)}
    beyond = ring.across(products[1, 1].astype(jnp.bfloat16), top)
    beside = ring.across(products[0, 1].astype(jnp.bfloat16), top)
    away = ring.between(add(products[1, 0], beyond), 2)
    return products[0, 0] + beside.astype(jnp.float32) + away.astype(jnp.float32)


def local(
    hidden_rows,
    token_embed,
    first_routes,
    first_gates,
    first_gate_up,
    first_down,
    second_routes,
    second_gates,
    second_gate_up,
    second_down,
    hidden_gain,
    embed_gain,
    merge_weight,
):
    ring = Ring()
    width = hidden_rows.shape[1]
    lanes = gate_lanes([(first_routes, first_gates), (second_routes, second_gates)])
    top = first_routes.shape[1]
    second_columns = {}

    def first_work(slot, chunk):
        second_columns[slot] = gate_column(ring, chunk[:, width:], 1, top)
        gates = gate_column(ring, chunk[:, width:], 0, top)
        return expert(chunk[:, :width], gates, first_gate_up[0], first_down[0])

    def second_work(slot, chunk):
        return expert(chunk, second_columns[slot], second_gate_up[0], second_down[0])

    first, gathered, summed = routed(ring, jnp.concatenate([hidden_rows, lanes], axis=1), first_work)
    weight = shared_weight(ring, after(merge_weight, gathered), summed)
    after_first = (hidden_rows.astype(jnp.float32) + first).astype(jnp.bfloat16)
    merged_in = jnp.concatenate([normed(after_first, hidden_gain), normed(token_embed, embed_gain)], axis=1)
    merged = merge(ring, merged_in, weight)
    after_merge = (after_first.astype(jnp.float32) + jax.nn.silu(merged)).astype(jnp.bfloat16)
    second, _, _ = routed(ring, after_merge, second_work)
    return (after_merge.astype(jnp.float32) + second).astype(jnp.bfloat16)


def solution(mesh):
    rows = P(("groups", "inner"), None)
    weight = P("inner", None, None)
    return jax.shard_map(
        local,
        mesh=mesh,
        in_specs=(rows, rows, rows, rows, weight, weight, rows, rows, weight, weight, P(), P(), P("inner", None)),
        out_specs=rows,
        check_vma=False,
    )
```

```python
import jax
import jax.numpy as jnp
from jax import lax
from jax.sharding import PartitionSpec as P

EPSILON = 1e-06
PLANES = 4


class Ring:
    def __init__(self):
        self.size = lax.axis_size("inner")
        self.plane = self.size // PLANES
        self.me = lax.axis_index("inner")
        self.z = self.me // self.plane
        self.inside = (self.z == 1) | (self.z == 2)
        self.bits = []
        bit = self.plane // 2
        while bit:
            self.bits.append(bit)
            bit //= 2

    def send(self, values, pairs):
        perm = [(a * self.plane + i, b * self.plane + i) for a, b in pairs for i in range(self.plane)]
        return lax.ppermute(values, "inner", perm)

    def between(self, values, slot):
        return self.send(values, [(p, p ^ slot) for p in range(PLANES)]) if slot else values

    def across(self, values, bit):
        return lax.ppermute(values, "inner", [(d, d ^ bit) for d in range(self.size)])

    def high(self, bit):
        return (self.me // bit) % 2 == 1


def after(values, *others):
    return lax.optimization_barrier((values, *others))[0]


def add(*terms):
    return sum(t.astype(jnp.float32) for t in terms).astype(jnp.bfloat16)


def within_plane(ring, chunk):
    for bit in reversed(ring.bits[1:]):
        rows = chunk.shape[0] // 2
        chunk = add(chunk[:rows], ring.across(chunk[rows:], bit))
    return chunk


def plane_sums(ring, part):
    return sum(ring.between(part(slot), slot).astype(jnp.float32) for slot in (0, 3, 2, 1))


def gate_lanes(layers):
    pieces = []
    for routes, gates in layers:
        high = gates.astype(jnp.bfloat16).astype(jnp.float32)
        pieces += [routes.astype(jnp.float32), high, gates - high]
    top = pieces[0].shape[1]
    width = -(-top * len(pieces) // 128) * 128
    placed = [jnp.pad(p, ((0, 0), (i * top, width - (i + 1) * top))) for i, p in enumerate(pieces)]
    return sum(placed).astype(jnp.bfloat16)


def gate_column(ring, lanes, layer, top):
    named, high, low = (lanes[:, (3 * layer + i) * top :][:, :top].astype(jnp.float32) for i in range(3))
    return jnp.sum(jnp.where(named == ring.me.astype(jnp.float32), high + low, 0.0), axis=1, keepdims=True)


def normed(values, gain):
    widened = values.astype(jnp.float32)
    inverse = lax.rsqrt(jnp.mean(widened * widened, axis=-1, keepdims=True) + EPSILON)
    return (widened * inverse * gain).astype(jnp.bfloat16)


def expert(rows, gates, gate_up, down):
    width = down.shape[0]
    projected = jnp.dot(rows, gate_up, preferred_element_type=jnp.float32)
    hidden = (jax.nn.silu(projected[:, :width]) * projected[:, width:]).astype(jnp.bfloat16)
    out = jnp.dot(hidden, down, preferred_element_type=jnp.float32)
    return (out * gates).astype(jnp.bfloat16)


def routed(ring, rows, work):
    top = ring.bits[0]
    columns = {0: rows, 1: ring.between(rows, 1)}
    crossed = {0: ring.across(rows, top)}
    middle = ring.send(rows, [(1, 2), (2, 1)])
    near = ring.send(middle, [(1, 0), (2, 3)])
    far = ring.send(columns[1], [(1, 2), (2, 1)])
    ends = ring.send(after(rows, columns[1], middle), [(0, 3), (3, 0)])
    columns[2] = jnp.where(ring.inside, far, near)
    columns[3] = jnp.where(ring.inside, middle, ends)
    for slot in (1, 2, 3):
        crossed[slot] = ring.across(columns[slot], top)

    def chunk(slot, *ties):
        values = after(jnp.concatenate([columns[slot], crossed[slot]], axis=0), *ties)
        for bit in ring.bits[1:]:
            values = jnp.concatenate([values, ring.across(values, bit)], axis=0)
        return values

    own = rows.shape[0]
    halves = {}
    back = {}

    def turn(slot, rows, *ties):
        done = work(slot, after(rows, *ties))
        halves[slot] = within_plane(ring, done)
        return done

    def swap(slot, *ties):
        back[slot] = ring.across(after(halves[slot][own:], *ties), top)
        parts[slot] = add(halves[slot][:own], back[slot])

    parts = {}
    last = [columns[3]]
    for slot in (0, 1, 2):
        last = [turn(slot, chunk(slot), *last)]
    turn(3, chunk(3, *last), halves[2])
    swap(2)
    swap(3)
    swap(1, halves[3], back[2])
    swap(0, halves[3], back[3])
    sums = plane_sums(ring, lambda slot: parts[slot])
    return sums, columns[3], back[3]


def shared_weight(ring, weight, groups, begin, swap):
    if groups % 2:
        other = after(ring.between(after(weight, begin), 1), swap)
    else:
        rows = weight.shape[0] // 2
        odd = lax.axis_index("groups") % 2
        sent = lax.dynamic_slice_in_dim(weight, odd * rows, rows, axis=0)
        here = after(ring.between(after(sent, begin), 1), swap)
        there = lax.ppermute(here, "groups", [(g, g ^ 1) for g in range(groups)])
        other = jnp.where(odd == 0, jnp.concatenate([here, there]), jnp.concatenate([there, here]))
    held = jnp.where(ring.z % 2 == 1, jnp.stack([other, weight]), jnp.stack([weight, other]))
    for i, bit in enumerate(ring.bits[1:]):
        other = ring.across(held, bit)
        axis = i + 1
        held = jnp.where(ring.high(bit), jnp.stack([other, held], axis), jnp.stack([held, other], axis))
    return held.reshape(ring.plane * weight.shape[0], weight.shape[1])


def merge(ring, merged_in, weight):
    top = ring.bits[0]
    share = merged_in.shape[1] // (2 * PLANES)
    steps = ((1, 1), (1, 0), (0, 1), (0, 0))
    pieces = []
    for far, side in steps:
        start = (2 * (ring.z // 2 ^ far) * 2 + (ring.high(top).astype(jnp.int32) ^ side)) * share
        halves = [lax.dynamic_slice_in_dim(merged_in, start + low * 2 * share, share, axis=1) for low in range(2)]
        piece = jnp.concatenate(halves, axis=1)
        crossing = far * 2 * ring.plane + side * top
        pieces.append(ring.across(piece, crossing) if crossing else piece)
    pieces[0] = after(pieces[0], *pieces[1:3])
    products = {s: jnp.dot(p, weight, preferred_element_type=jnp.float32) for s, p in zip(steps, pieces)}
    beyond = ring.across(products[1, 1].astype(jnp.bfloat16), top)
    beside = ring.across(products[0, 1].astype(jnp.bfloat16), top)
    away = ring.between(add(products[1, 0], beyond), 2)
    return products[0, 0] + beside.astype(jnp.float32) + away.astype(jnp.float32)


def local(
    hidden_rows,
    token_embed,
    first_routes,
    first_gates,
    first_gate_up,
    first_down,
    second_routes,
    second_gates,
    second_gate_up,
    second_down,
    hidden_gain,
    embed_gain,
    merge_weight,
):
    ring = Ring()
    width = hidden_rows.shape[1]
    lanes = gate_lanes([(first_routes, first_gates), (second_routes, second_gates)])
    top = first_routes.shape[1]
    second_columns = {}

    def first_work(slot, chunk):
        second_columns[slot] = gate_column(ring, chunk[:, width:], 1, top)
        gates = gate_column(ring, chunk[:, width:], 0, top)
        return expert(chunk[:, :width], gates, first_gate_up[0], first_down[0])

    def second_work(slot, chunk):
        return expert(chunk, second_columns[slot], second_gate_up[0], second_down[0])

    first, gathered, summed = routed(ring, jnp.concatenate([hidden_rows, lanes], axis=1), first_work)
    weight = shared_weight(ring, merge_weight, lax.axis_size("groups"), gathered, summed)
    after_first = (hidden_rows.astype(jnp.float32) + first).astype(jnp.bfloat16)
    merged_in = jnp.concatenate([normed(after_first, hidden_gain), normed(token_embed, embed_gain)], axis=1)
    merged = merge(ring, merged_in, weight)
    after_merge = (after_first.astype(jnp.float32) + jax.nn.silu(merged)).astype(jnp.bfloat16)
    second, _, _ = routed(ring, after_merge, second_work)
    return (after_merge.astype(jnp.float32) + second).astype(jnp.bfloat16)


def solution(mesh):
    rows = P(("groups", "inner"), None)
    weight = P("inner", None, None)
    return jax.shard_map(
        local,
        mesh=mesh,
        in_specs=(rows, rows, rows, rows, weight, weight, rows, rows, weight, weight, P(), P(), P("inner", None)),
        out_specs=rows,
        check_vma=False,
    )
```

```python
import jax
import jax.numpy as jnp
from jax import lax
from jax.sharding import PartitionSpec as P

EPSILON = 1e-06
PLANES = 4


class Ring:
    def __init__(self):
        self.size = lax.axis_size("inner")
        self.plane = self.size // PLANES
        self.me = lax.axis_index("inner")
        self.z = self.me // self.plane
        self.inside = (self.z == 1) | (self.z == 2)
        self.bits = []
        bit = self.plane // 2
        while bit:
            self.bits.append(bit)
            bit //= 2

    def send(self, values, pairs):
        perm = [(a * self.plane + i, b * self.plane + i) for a, b in pairs for i in range(self.plane)]
        return lax.ppermute(values, "inner", perm)

    def between(self, values, slot):
        return self.send(values, [(p, p ^ slot) for p in range(PLANES)]) if slot else values

    def across(self, values, bit):
        return lax.ppermute(values, "inner", [(d, d ^ bit) for d in range(self.size)])

    def high(self, bit):
        return (self.me // bit) % 2 == 1


def after(values, *others):
    return lax.optimization_barrier((values, *others))[0]


def add(*terms):
    return sum(t.astype(jnp.float32) for t in terms).astype(jnp.bfloat16)


def within_plane(ring, chunk):
    for bit in reversed(ring.bits[1:-1]):
        rows = chunk.shape[0] // 2
        chunk = add(chunk[:rows], ring.across(chunk[rows:], bit))
    return chunk


def plane_sums(ring, part):
    return sum(ring.between(part(slot), slot).astype(jnp.float32) for slot in (0, 3, 2, 1))


def gate_lanes(layers):
    pieces = []
    for routes, gates in layers:
        high = gates.astype(jnp.bfloat16).astype(jnp.float32)
        pieces += [routes.astype(jnp.float32), high, gates - high]
    top = pieces[0].shape[1]
    width = -(-top * len(pieces) // 128) * 128
    placed = [jnp.pad(p, ((0, 0), (i * top, width - (i + 1) * top))) for i, p in enumerate(pieces)]
    return sum(placed).astype(jnp.bfloat16)


def gate_column(lanes, who, layer, top):
    named, high, low = (lanes[:, (3 * layer + i) * top :][:, :top].astype(jnp.float32) for i in range(3))
    return jnp.sum(jnp.where(named == who.astype(jnp.float32), high + low, 0.0), axis=1, keepdims=True)


def normed(values, gain):
    widened = values.astype(jnp.float32)
    inverse = lax.rsqrt(jnp.mean(widened * widened, axis=-1, keepdims=True) + EPSILON)
    return (widened * inverse * gain).astype(jnp.bfloat16)


def two_experts(rows, gates, weights):
    total = 0.0
    for gate, (gate_up, down) in zip(gates, weights):
        width = down.shape[0]
        projected = jnp.dot(rows, gate_up, preferred_element_type=jnp.float32)
        hidden = jax.nn.silu(projected[:, :width]) * projected[:, width:] * gate
        total = total + jnp.dot(hidden.astype(jnp.bfloat16), down, preferred_element_type=jnp.float32)
    return total.astype(jnp.bfloat16)


def routed(ring, rows, work):
    top = ring.bits[0]
    columns = {0: rows, 1: ring.between(rows, 1)}
    crossed = {0: ring.across(rows, top)}
    middle = ring.send(rows, [(1, 2), (2, 1)])
    ends = ring.send(rows, [(0, 3), (3, 0)])
    near = ring.send(middle, [(1, 0), (2, 3)])
    far = ring.send(columns[1], [(1, 2), (2, 1)])
    columns[3] = jnp.where(ring.inside, middle, ends)
    columns[2] = jnp.where(ring.inside, far, near)
    crossed[1] = ring.across(after(columns[1], middle, crossed[0]), top)
    crossed[3] = ring.across(columns[3], top)
    crossed[2] = ring.across(columns[2], top)

    def chunk(*slots):
        parts = []
        for slot in slots:
            part = jnp.concatenate([columns[slot], crossed[slot]], axis=0)
            for bit in ring.bits[1:-1]:
                part = jnp.concatenate([part, ring.across(part, bit)], axis=0)
            parts.append(part)
        return jnp.concatenate(parts, axis=0)

    both = work((0, 1), after(chunk(0, 1), columns[2]))
    third = work((3,), after(chunk(3), both))
    halves = {3: within_plane(ring, third)}
    last = work((2,), after(chunk(2), halves[3]))
    count = both.shape[0] // 2
    for slot, done in ((2, last), (1, both[count:]), (0, both[:count])):
        halves[slot] = within_plane(ring, done)

    own = rows.shape[0]
    back = {}
    for slot, ties in ((3, []), (2, []), (1, [3]), (0, [2])):
        away = after(halves[slot][own:], *[back[t] for t in ties], *([halves[2]] if ties else []))
        back[slot] = ring.across(away, top)
    sums = plane_sums(ring, lambda slot: add(halves[slot][:own], back[slot]))
    return sums, [crossed[1], crossed[2], back[2]]


def other_half(ring, weight, groups, ties):
    top = ring.bits[0]
    rows = weight.shape[0] // 2
    odd = lax.axis_index("groups") % 2
    pieces = []
    for piece, (begin, swap) in enumerate(ties):
        if groups % 2:
            pieces.append(ring.across(after(weight[piece * rows : (piece + 1) * rows], *begin), top))
            continue
        sent = lax.dynamic_slice_in_dim(weight, piece * rows + odd * (rows // 2), rows // 2, axis=0)
        here = after(ring.across(after(sent, *begin), top), *swap)
        there = lax.ppermute(here, "groups", [(g, g ^ 1) for g in range(groups)])
        pieces += [jnp.where(odd == 0, here, there), jnp.where(odd == 0, there, here)]
    return jnp.concatenate(pieces, axis=0)


def plane_weight(ring, weight, other):
    held = jnp.where(ring.high(ring.bits[0]), jnp.stack([other, weight]), jnp.stack([weight, other]))
    for i, bit in enumerate(ring.bits[1:]):
        other = ring.across(held, bit)
        axis = i + 1
        held = jnp.where(ring.high(bit), jnp.stack([other, held], axis), jnp.stack([held, other], axis))
    return held.reshape(ring.plane * weight.shape[0], weight.shape[1])


def merge(ring, merged_in, weight):
    share = merged_in.shape[1] // PLANES
    products = {}
    for slot in (2, 3, 1, 0):
        piece = lax.dynamic_slice_in_dim(merged_in, (ring.z ^ slot) * share, share, axis=1)
        products[slot] = jnp.dot(ring.between(piece, slot), weight, preferred_element_type=jnp.float32)
        if slot:
            products[slot] = products[slot].astype(jnp.bfloat16)
    return plane_sums(ring, lambda slot: products[slot])


def local(
    hidden_rows,
    token_embed,
    first_routes,
    first_gates,
    first_gate_up,
    first_down,
    second_routes,
    second_gates,
    second_gate_up,
    second_down,
    hidden_gain,
    embed_gain,
    merge_weight,
):
    ring = Ring()
    width = hidden_rows.shape[1]
    lanes = gate_lanes([(first_routes, first_gates), (second_routes, second_gates)])
    top = first_routes.shape[1]
    people = (ring.me, ring.me ^ 1)
    second_columns = {}

    def pair(gate_up, down, *ties):
        mine = (gate_up[0], down[0])
        return mine, tuple(ring.across(after(w, *ties), ring.bits[-1]) for w in mine)

    first_pair = pair(first_gate_up, first_down)

    def first_work(slots, chunk):
        lanes = chunk[:, width:]
        second_columns[slots] = [gate_column(lanes, who, 1, top) for who in people]
        return two_experts(chunk[:, :width], [gate_column(lanes, who, 0, top) for who in people], first_pair)

    def second_work(slots, chunk):
        return two_experts(chunk, second_columns[slots], second_pair)

    first, steps = routed(ring, jnp.concatenate([hidden_rows, lanes], axis=1), first_work)
    second_pair = pair(second_gate_up, second_down, steps[1])
    ties = [([], [steps[0]]), ([steps[1]], [steps[2]])]
    weight = plane_weight(ring, merge_weight, other_half(ring, merge_weight, lax.axis_size("groups"), ties))
    after_first = (hidden_rows.astype(jnp.float32) + first).astype(jnp.bfloat16)
    merged_in = jnp.concatenate([normed(after_first, hidden_gain), normed(token_embed, embed_gain)], axis=1)
    merged = merge(ring, merged_in, weight)
    after_merge = (after_first.astype(jnp.float32) + jax.nn.silu(merged)).astype(jnp.bfloat16)
    second, _ = routed(ring, after_merge, second_work)
    return (after_merge.astype(jnp.float32) + second).astype(jnp.bfloat16)


def solution(mesh):
    rows = P(("groups", "inner"), None)
    weight = P("inner", None, None)
    return jax.shard_map(
        local,
        mesh=mesh,
        in_specs=(rows, rows, rows, rows, weight, weight, rows, rows, weight, weight, P(), P(), P("inner", None)),
        out_specs=rows,
        check_vma=False,
    )
```

```python
import jax
import jax.numpy as jnp
from jax import lax
from jax.sharding import PartitionSpec as P

EPSILON = 1e-06
PLANES = 4


class Ring:
    def __init__(self):
        self.size = lax.axis_size("inner")
        self.plane = self.size // PLANES
        self.me = lax.axis_index("inner")
        self.z = self.me // self.plane
        self.inside = (self.z == 1) | (self.z == 2)
        self.bits = []
        bit = self.plane // 2
        while bit:
            self.bits.append(bit)
            bit //= 2

    def send(self, values, pairs):
        perm = [(a * self.plane + i, b * self.plane + i) for a, b in pairs for i in range(self.plane)]
        return lax.ppermute(values, "inner", perm)

    def between(self, values, slot):
        return self.send(values, [(p, p ^ slot) for p in range(PLANES)]) if slot else values

    def across(self, values, bit):
        return lax.ppermute(values, "inner", [(d, d ^ bit) for d in range(self.size)])

    def high(self, bit):
        return (self.me // bit) % 2 == 1


def after(values, *others):
    return lax.optimization_barrier((values, *others))[0]


def add(*terms):
    return sum(t.astype(jnp.float32) for t in terms).astype(jnp.bfloat16)


def within_plane(ring, chunk, bits):
    for bit in reversed(bits):
        rows = chunk.shape[0] // 2
        chunk = add(chunk[:rows], ring.across(chunk[rows:], bit))
    return chunk


def plane_sums(ring, part):
    return sum(ring.between(part(slot), slot).astype(jnp.float32) for slot in (0, 3, 2, 1))


def gate_lanes(layers):
    pieces = []
    for routes, gates in layers:
        high = gates.astype(jnp.bfloat16).astype(jnp.float32)
        pieces += [routes.astype(jnp.float32), high, gates - high]
    top = pieces[0].shape[1]
    width = -(-top * len(pieces) // 128) * 128
    placed = [jnp.pad(p, ((0, 0), (i * top, width - (i + 1) * top))) for i, p in enumerate(pieces)]
    return sum(placed).astype(jnp.bfloat16)


def gate_column(lanes, who, layer, top):
    named, high, low = (lanes[:, (3 * layer + i) * top :][:, :top].astype(jnp.float32) for i in range(3))
    return jnp.sum(jnp.where(named == who.astype(jnp.float32), high + low, 0.0), axis=1, keepdims=True)


def normed(values, gain):
    widened = values.astype(jnp.float32)
    inverse = lax.rsqrt(jnp.mean(widened * widened, axis=-1, keepdims=True) + EPSILON)
    return (widened * inverse * gain).astype(jnp.bfloat16)


def experts(rows, gates, weights):
    total = 0.0
    for gate, (gate_up, down) in zip(gates, weights):
        width = down.shape[0]
        projected = jnp.dot(rows, gate_up, preferred_element_type=jnp.float32)
        hidden = jax.nn.silu(projected[:, :width]) * projected[:, width:] * gate
        total = total + jnp.dot(hidden.astype(jnp.bfloat16), down, preferred_element_type=jnp.float32)
    return total.astype(jnp.bfloat16)


def routed(ring, rows, work, paired):
    top = ring.bits[0]
    below = ring.bits[1:-1] if paired else ring.bits[1:]
    columns = {0: rows}
    for slot in (1, 3, 2):
        columns[slot] = ring.between(rows, slot)
    crossed = {slot: ring.across(columns[slot], top) for slot in (0, 1)}
    crossed[3] = ring.across(after(columns[3], crossed[1]), top)
    crossed[2] = ring.across(after(columns[2], crossed[3]), top)

    def chunk(slot, *ties):
        part = after(jnp.concatenate([columns[slot], crossed[slot]], axis=0), *ties)
        for bit in below:
            part = jnp.concatenate([part, ring.across(part, bit)], axis=0)
        return part

    def halve(done):
        return within_plane(ring, done, below)

    halves = {}
    if paired:
        both = work((0, 1), after(jnp.concatenate([chunk(0), chunk(1)], axis=0), crossed[3]))
        third = work((3,), after(chunk(3), both))
        halves[3] = halve(third)
        last = work((2,), after(chunk(2), halves[3]))
        count = both.shape[0] // 2
        done = {0: both[:count], 1: both[count:]}
    else:
        done = {}
        ties = [crossed[3]]
        for slot in (0, 1, 3):
            done[slot] = work((slot,), after(chunk(slot), *ties))
            ties = [done[slot]]
        halves[3] = halve(done[3])
        last = work((2,), after(chunk(2, *ties), halves[3]))
    halves[2] = halve(last)
    for slot in (1, 0):
        halves[slot] = halve(done[slot])

    own = rows.shape[0]
    back = {}
    for slot, ties in ((3, []), (2, []), (1, [3]), (0, [2])):
        away = after(halves[slot][own:], *[back[t] for t in ties], *([halves[2]] if ties else []))
        back[slot] = ring.across(away, top)
    sums = plane_sums(ring, lambda slot: add(halves[slot][:own], back[slot]))
    return sums, [crossed[1], crossed[2], back[2]]


def other_half(ring, weight, groups, ties):
    top = ring.bits[0]
    rows = weight.shape[0] // 2
    odd = lax.axis_index("groups") % 2
    pieces = []
    for piece, (begin, swap) in enumerate(ties):
        if groups % 2:
            pieces.append(ring.across(after(weight[piece * rows : (piece + 1) * rows], *begin), top))
            continue
        sent = lax.dynamic_slice_in_dim(weight, piece * rows + odd * (rows // 2), rows // 2, axis=0)
        here = after(ring.across(after(sent, *begin), top), *swap)
        there = lax.ppermute(here, "groups", [(g, g ^ 1) for g in range(groups)])
        pieces += [jnp.where(odd == 0, here, there), jnp.where(odd == 0, there, here)]
    return jnp.concatenate(pieces, axis=0)


def plane_weight(ring, weight, other):
    held = jnp.where(ring.high(ring.bits[0]), jnp.stack([other, weight]), jnp.stack([weight, other]))
    for i, bit in enumerate(ring.bits[1:]):
        other = ring.across(held, bit)
        axis = i + 1
        held = jnp.where(ring.high(bit), jnp.stack([other, held], axis), jnp.stack([held, other], axis))
    return held.reshape(ring.plane * weight.shape[0], weight.shape[1])


def merge(ring, merged_in, weight):
    share = merged_in.shape[1] // PLANES
    products = {}
    for slot in (2, 3, 1, 0):
        piece = lax.dynamic_slice_in_dim(merged_in, (ring.z ^ slot) * share, share, axis=1)
        products[slot] = jnp.dot(ring.between(piece, slot), weight, preferred_element_type=jnp.float32)
        if slot:
            products[slot] = products[slot].astype(jnp.bfloat16)
    return plane_sums(ring, lambda slot: products[slot])


def local(
    hidden_rows,
    token_embed,
    first_routes,
    first_gates,
    first_gate_up,
    first_down,
    second_routes,
    second_gates,
    second_gate_up,
    second_down,
    hidden_gain,
    embed_gain,
    merge_weight,
):
    ring = Ring()
    width = hidden_rows.shape[1]
    lanes = gate_lanes([(first_routes, first_gates), (second_routes, second_gates)])
    top = first_routes.shape[1]
    people = (ring.me, ring.me ^ 1)
    second_lanes = {}

    def first_work(slots, chunk):
        lanes = chunk[:, width:]
        second_lanes[slots[0]] = lanes[: chunk.shape[0] // 2]
        return experts(
            chunk[:, :width], [gate_column(lanes, ring.me, 0, top)], [(first_gate_up[0], first_down[0])]
        )

    def second_work(slots, chunk):
        lanes = jnp.concatenate([second_lanes[slot] for slot in slots], axis=0)
        return experts(chunk, [gate_column(lanes, who, 1, top) for who in people], second_pair)

    first, steps = routed(ring, jnp.concatenate([hidden_rows, lanes], axis=1), first_work, False)
    mine = (second_gate_up[0], second_down[0])
    second_pair = (mine, tuple(ring.across(after(w, steps[1]), ring.bits[-1]) for w in mine))
    ties = [([], [steps[0]]), ([steps[1]], [steps[2]])]
    weight = plane_weight(ring, merge_weight, other_half(ring, merge_weight, lax.axis_size("groups"), ties))
    after_first = (hidden_rows.astype(jnp.float32) + first).astype(jnp.bfloat16)
    merged_in = jnp.concatenate([normed(after_first, hidden_gain), normed(token_embed, embed_gain)], axis=1)
    merged = merge(ring, merged_in, weight)
    after_merge = (after_first.astype(jnp.float32) + jax.nn.silu(merged)).astype(jnp.bfloat16)
    second, _ = routed(ring, after(after_merge, *second_pair[1]), second_work, True)
    return (after_merge.astype(jnp.float32) + second).astype(jnp.bfloat16)


def solution(mesh):
    rows = P(("groups", "inner"), None)
    weight = P("inner", None, None)
    return jax.shard_map(
        local,
        mesh=mesh,
        in_specs=(rows, rows, rows, rows, weight, weight, rows, rows, weight, weight, P(), P(), P("inner", None)),
        out_specs=rows,
        check_vma=False,
    )
```

```python
import jax
import jax.numpy as jnp
from jax import lax
from jax.sharding import PartitionSpec as P

EPSILON = 1e-06
PLANES = 4


class Ring:
    def __init__(self):
        self.size = lax.axis_size("inner")
        self.plane = self.size // PLANES
        self.me = lax.axis_index("inner")
        self.z = self.me // self.plane
        self.inside = (self.z == 1) | (self.z == 2)
        self.bits = []
        bit = self.plane // 2
        while bit:
            self.bits.append(bit)
            bit //= 2

    def send(self, values, pairs):
        perm = [(a * self.plane + i, b * self.plane + i) for a, b in pairs for i in range(self.plane)]
        return lax.ppermute(values, "inner", perm)

    def between(self, values, slot):
        return self.send(values, [(p, p ^ slot) for p in range(PLANES)]) if slot else values

    def across(self, values, bit):
        return lax.ppermute(values, "inner", [(d, d ^ bit) for d in range(self.size)])

    def high(self, bit):
        return (self.me // bit) % 2 == 1


def after(values, *others):
    return lax.optimization_barrier((values, *others))[0]


def add(*terms):
    return sum(t.astype(jnp.float32) for t in terms).astype(jnp.bfloat16)


def within_plane(ring, chunk, bits):
    for bit in reversed(bits):
        rows = chunk.shape[0] // 2
        chunk = add(chunk[:rows], ring.across(chunk[rows:], bit))
    return chunk


def plane_sums(ring, part):
    return sum(ring.between(part(slot), slot).astype(jnp.float32) for slot in (0, 3, 2, 1))


def gate_lanes(layers):
    pieces = []
    for routes, gates in layers:
        high = gates.astype(jnp.bfloat16).astype(jnp.float32)
        pieces += [routes.astype(jnp.float32), high, gates - high]
    top = pieces[0].shape[1]
    width = -(-top * len(pieces) // 128) * 128
    placed = [jnp.pad(p, ((0, 0), (i * top, width - (i + 1) * top))) for i, p in enumerate(pieces)]
    return sum(placed).astype(jnp.bfloat16)


def gate_column(lanes, who, layer, top):
    named, high, low = (lanes[:, (3 * layer + i) * top :][:, :top].astype(jnp.float32) for i in range(3))
    return jnp.sum(jnp.where(named == who.astype(jnp.float32), high + low, 0.0), axis=1, keepdims=True)


def normed(values, gain):
    widened = values.astype(jnp.float32)
    inverse = lax.rsqrt(jnp.mean(widened * widened, axis=-1, keepdims=True) + EPSILON)
    return (widened * inverse * gain).astype(jnp.bfloat16)


def experts(rows, gates, weights):
    total = 0.0
    for gate, (gate_up, down) in zip(gates, weights):
        width = down.shape[0]
        projected = jnp.dot(rows, gate_up, preferred_element_type=jnp.float32)
        hidden = jax.nn.silu(projected[:, :width]) * projected[:, width:] * gate
        total = total + jnp.dot(hidden.astype(jnp.bfloat16), down, preferred_element_type=jnp.float32)
    return total.astype(jnp.bfloat16)


def routed(ring, rows, work, paired):
    top = ring.bits[0]
    below = ring.bits[1:-1] if paired else ring.bits[1:]
    columns = {0: rows}
    for slot in (1, 3, 2):
        columns[slot] = ring.between(rows, slot)
    crossed = {slot: ring.across(columns[slot], top) for slot in (0, 1)}
    crossed[3] = ring.across(after(columns[3], crossed[1]), top)
    crossed[2] = ring.across(after(columns[2], crossed[3]), top)

    def chunk(slot, *ties):
        part = after(jnp.concatenate([columns[slot], crossed[slot]], axis=0), *ties)
        for bit in below:
            part = jnp.concatenate([part, ring.across(part, bit)], axis=0)
        return part

    def halve(done):
        return within_plane(ring, done, below)

    halves = {}
    if paired:
        third = work((3,), after(chunk(3), crossed[3]))
        halves[3] = halve(third)
        both = work((0, 1), after(jnp.concatenate([chunk(0), chunk(1)], axis=0), third))
        last = work((2,), after(chunk(2), both, halves[3]))
        count = both.shape[0] // 2
        done = {0: both[:count], 1: both[count:]}
    else:
        done = {}
        ties = [crossed[3]]
        for slot in (0, 1, 3):
            done[slot] = work((slot,), after(chunk(slot), *ties))
            ties = [done[slot]]
        halves[3] = halve(done[3])
        last = work((2,), after(chunk(2, *ties), halves[3]))
    halves[2] = halve(last)
    for slot in (1, 0):
        halves[slot] = halve(done[slot])

    own = rows.shape[0]
    back = {}
    for slot, ties in ((3, []), (2, []), (1, [3]), (0, [2])):
        away = after(halves[slot][own:], *[back[t] for t in ties], *([halves[2]] if ties else []))
        back[slot] = ring.across(away, top)
    sums = plane_sums(ring, lambda slot: add(halves[slot][:own], back[slot]))
    return sums, [crossed[1], crossed[2], back[2]]


def other_half(ring, weight, groups, ties):
    top = ring.bits[0]
    rows = weight.shape[0] // 2
    odd = lax.axis_index("groups") % 2
    pieces = []
    for piece, (begin, swap) in enumerate(ties):
        if groups % 2:
            pieces.append(ring.across(after(weight[piece * rows : (piece + 1) * rows], *begin), top))
            continue
        sent = lax.dynamic_slice_in_dim(weight, piece * rows + odd * (rows // 2), rows // 2, axis=0)
        here = after(ring.across(after(sent, *begin), top), *swap)
        there = lax.ppermute(here, "groups", [(g, g ^ 1) for g in range(groups)])
        pieces += [jnp.where(odd == 0, here, there), jnp.where(odd == 0, there, here)]
    return jnp.concatenate(pieces, axis=0)


def plane_weight(ring, weight, other):
    held = jnp.where(ring.high(ring.bits[0]), jnp.stack([other, weight]), jnp.stack([weight, other]))
    for i, bit in enumerate(ring.bits[1:]):
        other = ring.across(held, bit)
        axis = i + 1
        held = jnp.where(ring.high(bit), jnp.stack([other, held], axis), jnp.stack([held, other], axis))
    return held.reshape(ring.plane * weight.shape[0], weight.shape[1])


def merge(ring, merged_in, weight):
    share = merged_in.shape[1] // PLANES
    products = {}
    for slot in (2, 3, 1, 0):
        piece = lax.dynamic_slice_in_dim(merged_in, (ring.z ^ slot) * share, share, axis=1)
        products[slot] = jnp.dot(ring.between(piece, slot), weight, preferred_element_type=jnp.float32)
        if slot:
            products[slot] = products[slot].astype(jnp.bfloat16)
    return plane_sums(ring, lambda slot: products[slot])


def local(
    hidden_rows,
    token_embed,
    first_routes,
    first_gates,
    first_gate_up,
    first_down,
    second_routes,
    second_weights,
    second_gate_up,
    second_down,
    hidden_gain,
    embed_gain,
    merge_weight,
):
    ring = Ring()
    width = hidden_rows.shape[1]
    lanes = gate_lanes([(first_routes, first_gates), (second_routes, second_weights)])
    top = first_routes.shape[1]
    people = (ring.me, ring.me ^ 1)
    second_gates = {}

    def first_work(slots, chunk):
        lanes = chunk[:, width:]
        paired = lanes[: chunk.shape[0] // 2]
        second_gates[slots[0]] = [gate_column(paired, who, 1, top) for who in people]
        return experts(
            chunk[:, :width], [gate_column(lanes, ring.me, 0, top)], [(first_gate_up[0], first_down[0])]
        )

    def second_work(slots, chunk):
        gates = [jnp.concatenate([second_gates[slot][i] for slot in slots], axis=0) for i in range(2)]
        return experts(chunk, gates, second_pair)

    first, steps = routed(ring, jnp.concatenate([hidden_rows, lanes], axis=1), first_work, False)
    mine = (second_gate_up[0], second_down[0])
    second_pair = (mine, tuple(ring.across(after(w, steps[1]), ring.bits[-1]) for w in mine))
    ties = [([], [steps[0]]), ([steps[1]], [steps[2]])]
    weight = plane_weight(ring, merge_weight, other_half(ring, merge_weight, lax.axis_size("groups"), ties))
    after_first = (hidden_rows.astype(jnp.float32) + first).astype(jnp.bfloat16)
    merged_in = jnp.concatenate([normed(after_first, hidden_gain), normed(token_embed, embed_gain)], axis=1)
    merged = merge(ring, merged_in, after(weight, *second_pair[1], *[g for slot in range(PLANES) for g in second_gates[slot]]))
    after_merge = (after_first.astype(jnp.float32) + jax.nn.silu(merged)).astype(jnp.bfloat16)
    second, _ = routed(ring, after_merge, second_work, True)
    return (after_merge.astype(jnp.float32) + second).astype(jnp.bfloat16)


def solution(mesh):
    rows = P(("groups", "inner"), None)
    weight = P("inner", None, None)
    return jax.shard_map(
        local,
        mesh=mesh,
        in_specs=(rows, rows, rows, rows, weight, weight, rows, rows, weight, weight, P(), P(), P("inner", None)),
        out_specs=rows,
        check_vma=False,
    )
```

```python
import jax
import jax.numpy as jnp
from jax import lax
from jax.sharding import PartitionSpec as P

EPSILON = 1e-06
PLANES = 4


class Ring:
    def __init__(self):
        self.size = lax.axis_size("inner")
        self.plane = self.size // PLANES
        self.me = lax.axis_index("inner")
        self.z = self.me // self.plane
        self.inside = (self.z == 1) | (self.z == 2)
        self.bits = []
        bit = self.plane // 2
        while bit:
            self.bits.append(bit)
            bit //= 2

    def send(self, values, pairs):
        perm = [(a * self.plane + i, b * self.plane + i) for a, b in pairs for i in range(self.plane)]
        return lax.ppermute(values, "inner", perm)

    def between(self, values, slot):
        return self.send(values, [(p, p ^ slot) for p in range(PLANES)]) if slot else values

    def across(self, values, bit):
        return lax.ppermute(values, "inner", [(d, d ^ bit) for d in range(self.size)])

    def high(self, bit):
        return (self.me // bit) % 2 == 1


def after(values, *others):
    return lax.optimization_barrier((values, *others))[0]


def add(*terms):
    return sum(t.astype(jnp.float32) for t in terms).astype(jnp.bfloat16)


def within_plane(ring, chunk, bits):
    for bit in reversed(bits):
        rows = chunk.shape[0] // 2
        chunk = add(chunk[:rows], ring.across(chunk[rows:], bit))
    return chunk


def plane_sums(ring, part):
    return sum(ring.between(part(slot), slot).astype(jnp.float32) for slot in (0, 3, 2, 1))


def gate_lanes(layers):
    pieces = []
    for routes, gates in layers:
        high = gates.astype(jnp.bfloat16).astype(jnp.float32)
        pieces += [routes.astype(jnp.float32), high, gates - high]
    top = pieces[0].shape[1]
    width = -(-top * len(pieces) // 128) * 128
    placed = [jnp.pad(p, ((0, 0), (i * top, width - (i + 1) * top))) for i, p in enumerate(pieces)]
    return sum(placed).astype(jnp.bfloat16)


def gate_column(lanes, who, layer, top):
    named, high, low = (lanes[:, (3 * layer + i) * top :][:, :top].astype(jnp.float32) for i in range(3))
    return jnp.sum(jnp.where(named == who.astype(jnp.float32), high + low, 0.0), axis=1, keepdims=True)


def normed(values, gain):
    widened = values.astype(jnp.float32)
    inverse = lax.rsqrt(jnp.mean(widened * widened, axis=-1, keepdims=True) + EPSILON)
    return (widened * inverse * gain).astype(jnp.bfloat16)


def experts(rows, gates, weights):
    total = 0.0
    for gate, (gate_up, down) in zip(gates, weights):
        width = down.shape[0]
        projected = jnp.dot(rows, gate_up, preferred_element_type=jnp.float32)
        hidden = jax.nn.silu(projected[:, :width]) * projected[:, width:] * gate
        total = total + jnp.dot(hidden.astype(jnp.bfloat16), down, preferred_element_type=jnp.float32)
    return total.astype(jnp.bfloat16)


def routed(ring, rows, work, paired):
    top = ring.bits[0]
    below = ring.bits[1:-1] if paired else ring.bits[1:]
    columns = {0: rows}
    for slot in (1, 3, 2):
        columns[slot] = ring.between(rows, slot)
    crossed = {slot: ring.across(columns[slot], top) for slot in (0, 1)}
    crossed[3] = ring.across(after(columns[3], crossed[1]), top)
    crossed[2] = ring.across(after(columns[2], crossed[3]), top)

    def chunk(slot, *ties):
        part = after(jnp.concatenate([columns[slot], crossed[slot]], axis=0), *ties)
        for bit in below:
            part = jnp.concatenate([part, ring.across(part, bit)], axis=0)
        return part

    def halve(done):
        return within_plane(ring, done, below)

    halves = {}
    if paired:
        third = work((3,), after(chunk(3), crossed[3]))
        halves[3] = halve(third)
        both = work((0, 1), after(jnp.concatenate([chunk(0), chunk(1)], axis=0), third))
        last = work((2,), after(chunk(2), both, halves[3]))
        count = both.shape[0] // 2
        done = {0: both[:count], 1: both[count:]}
    else:
        done = {}
        ties = [crossed[3]]
        for slot in (0, 1, 3):
            done[slot] = work((slot,), after(chunk(slot), *ties))
            ties = [done[slot]]
        halves[3] = halve(done[3])
        last = work((2,), after(chunk(2, *ties), halves[3]))
    halves[2] = halve(last)
    for slot in (1, 0):
        halves[slot] = halve(done[slot])

    own = rows.shape[0]
    back = {}
    for slot, ties in ((3, []), (2, []), (1, [3]), (0, [2])):
        away = after(halves[slot][own:], *[back[t] for t in ties], *([halves[2]] if ties else []))
        back[slot] = ring.across(away, top)
    sums = plane_sums(ring, lambda slot: add(halves[slot][:own], back[slot]))
    return sums, [crossed[1], crossed[2], back[2]]


def other_half(ring, weight, groups, ties):
    top = ring.bits[0]
    rows = weight.shape[0] // 2
    odd = lax.axis_index("groups") % 2
    pieces = []
    for piece, (begin, swap) in enumerate(ties):
        if groups % 2:
            pieces.append(ring.across(after(weight[piece * rows : (piece + 1) * rows], *begin), top))
            continue
        sent = lax.dynamic_slice_in_dim(weight, piece * rows + odd * (rows // 2), rows // 2, axis=0)
        here = after(ring.across(after(sent, *begin), top), *swap)
        there = lax.ppermute(here, "groups", [(g, g ^ 1) for g in range(groups)])
        pieces += [jnp.where(odd == 0, here, there), jnp.where(odd == 0, there, here)]
    return jnp.concatenate(pieces, axis=0)


def plane_weight(ring, weight, other):
    held = jnp.where(ring.high(ring.bits[0]), jnp.stack([other, weight]), jnp.stack([weight, other]))
    for i, bit in enumerate(ring.bits[1:]):
        other = ring.across(held, bit)
        axis = i + 1
        held = jnp.where(ring.high(bit), jnp.stack([other, held], axis), jnp.stack([held, other], axis))
    return held.reshape(ring.plane * weight.shape[0], weight.shape[1])


def merge(ring, merged_in, weight):
    share = merged_in.shape[1] // PLANES
    products = {}
    for slot in (2, 3, 1, 0):
        piece = lax.dynamic_slice_in_dim(merged_in, (ring.z ^ slot) * share, share, axis=1)
        products[slot] = jnp.dot(ring.between(piece, slot), weight, preferred_element_type=jnp.float32)
        if slot:
            products[slot] = products[slot].astype(jnp.bfloat16)
    return plane_sums(ring, lambda slot: products[slot])


def local(
    hidden_rows,
    token_embed,
    first_routes,
    first_gates,
    first_gate_up,
    first_down,
    second_routes,
    second_weights,
    second_gate_up,
    second_down,
    hidden_gain,
    embed_gain,
    merge_weight,
):
    ring = Ring()
    width = hidden_rows.shape[1]
    lanes = gate_lanes([(first_routes, first_gates), (second_routes, second_weights)])
    top = first_routes.shape[1]
    people = (ring.me, ring.me ^ 1)
    second_gates = {}

    def first_work(slots, chunk):
        lanes = chunk[:, width:]
        paired = lanes[: chunk.shape[0] // 2]
        second_gates[slots[0]] = [gate_column(paired, who, 1, top) for who in people]
        return experts(
            chunk[:, :width], [gate_column(lanes, ring.me, 0, top)], [(first_gate_up[0], first_down[0])]
        )

    def second_work(slots, chunk):
        gates = [jnp.concatenate([second_gates[slot][i] for slot in slots], axis=0) for i in range(2)]
        return experts(chunk, gates, second_pair)

    first, steps = routed(ring, jnp.concatenate([hidden_rows, lanes], axis=1), first_work, False)
    mine = (second_gate_up[0], second_down[0])
    second_pair = (mine, tuple(ring.across(after(w, steps[1]), ring.bits[-1]) for w in mine))
    ties = [([], [steps[0]]), ([steps[1]], [steps[2]])]
    weight = plane_weight(ring, merge_weight, other_half(ring, merge_weight, lax.axis_size("groups"), ties))
    after_first = (hidden_rows.astype(jnp.float32) + first).astype(jnp.bfloat16)
    merged_in = jnp.concatenate([normed(after_first, hidden_gain), normed(token_embed, embed_gain)], axis=1)
    merged = merge(ring, merged_in, after(weight, *[g for slot in range(PLANES) for g in second_gates[slot]]))
    after_merge = (after_first.astype(jnp.float32) + jax.nn.silu(merged)).astype(jnp.bfloat16)
    second, _ = routed(ring, after(after_merge, *second_pair[1]), second_work, True)
    return (after_merge.astype(jnp.float32) + second).astype(jnp.bfloat16)


def solution(mesh):
    rows = P(("groups", "inner"), None)
    weight = P("inner", None, None)
    return jax.shard_map(
        local,
        mesh=mesh,
        in_specs=(rows, rows, rows, rows, weight, weight, rows, rows, weight, weight, P(), P(), P("inner", None)),
        out_specs=rows,
        check_vma=False,
    )
```

```python
import jax
import jax.numpy as jnp
from jax import lax
from jax.sharding import PartitionSpec as P

EPSILON = 1e-06
PLANES = 4


class Ring:
    def __init__(self):
        self.size = lax.axis_size("inner")
        self.plane = self.size // PLANES
        self.me = lax.axis_index("inner")
        self.z = self.me // self.plane
        self.inside = (self.z == 1) | (self.z == 2)
        self.bits = []
        bit = self.plane // 2
        while bit:
            self.bits.append(bit)
            bit //= 2

    def send(self, values, pairs):
        perm = [(a * self.plane + i, b * self.plane + i) for a, b in pairs for i in range(self.plane)]
        return lax.ppermute(values, "inner", perm)

    def between(self, values, slot):
        return self.send(values, [(p, p ^ slot) for p in range(PLANES)]) if slot else values

    def across(self, values, bit):
        return lax.ppermute(values, "inner", [(d, d ^ bit) for d in range(self.size)])

    def high(self, bit):
        return (self.me // bit) % 2 == 1


def after(values, *others):
    return lax.optimization_barrier((values, *others))[0]


def add(*terms):
    return sum(t.astype(jnp.float32) for t in terms).astype(jnp.bfloat16)


def within_plane(ring, chunk, bits):
    for bit in reversed(bits):
        rows = chunk.shape[0] // 2
        chunk = add(chunk[:rows], ring.across(chunk[rows:], bit))
    return chunk


def plane_sums(ring, part):
    return sum(ring.between(part(slot), slot).astype(jnp.float32) for slot in (0, 3, 2, 1))


def gate_lanes(layers):
    pieces = []
    for routes, gates in layers:
        high = gates.astype(jnp.bfloat16).astype(jnp.float32)
        pieces += [routes.astype(jnp.float32), high, gates - high]
    top = pieces[0].shape[1]
    width = -(-top * len(pieces) // 128) * 128
    placed = [jnp.pad(p, ((0, 0), (i * top, width - (i + 1) * top))) for i, p in enumerate(pieces)]
    return sum(placed).astype(jnp.bfloat16)


def gate_column(lanes, who, layer, top):
    named, high, low = (lanes[:, (3 * layer + i) * top :][:, :top].astype(jnp.float32) for i in range(3))
    return jnp.sum(jnp.where(named == who.astype(jnp.float32), high + low, 0.0), axis=1, keepdims=True)


def normed(values, gain):
    widened = values.astype(jnp.float32)
    inverse = lax.rsqrt(jnp.mean(widened * widened, axis=-1, keepdims=True) + EPSILON)
    return (widened * inverse * gain).astype(jnp.bfloat16)


def experts(rows, gates, weights):
    total = 0.0
    for gate, (gate_up, down) in zip(gates, weights):
        width = down.shape[0]
        projected = jnp.dot(rows, gate_up, preferred_element_type=jnp.float32)
        hidden = jax.nn.silu(projected[:, :width]) * projected[:, width:] * gate
        total = total + jnp.dot(hidden.astype(jnp.bfloat16), down, preferred_element_type=jnp.float32)
    return total.astype(jnp.bfloat16)


def routed(ring, rows, work, paired):
    top = ring.bits[0]
    below = ring.bits[1:-1] if paired else ring.bits[1:]
    columns = {0: rows}
    for slot in (1, 3, 2):
        columns[slot] = ring.between(rows, slot)
    crossed = {0: ring.across(rows, top)}
    crossed[1] = ring.across(after(columns[1], crossed[0]) if paired else columns[1], top)
    crossed[3] = ring.across(after(columns[3], crossed[1]), top)
    crossed[2] = ring.across(after(columns[2], crossed[3]), top)

    def chunk(slot, *ties):
        part = after(jnp.concatenate([columns[slot], crossed[slot]], axis=0), *ties)
        for bit in below:
            part = jnp.concatenate([part, ring.across(part, bit)], axis=0)
        return part

    def halve(done):
        return within_plane(ring, done, below)

    halves = {}
    if paired:
        both = work((3, 0), after(jnp.concatenate([chunk(3), chunk(0)], axis=0), crossed[3]))
        count = both.shape[0] // 2
        halves[3] = halve(both[:count])
        done = {0: both[count:], 1: work((1,), after(chunk(1), both))}
        last = work((2,), after(chunk(2), done[1], halves[3]))
    else:
        done = {}
        ties = [crossed[3]]
        for slot in (0, 1, 3):
            done[slot] = work((slot,), after(chunk(slot), *ties))
            ties = [done[slot]]
        halves[3] = halve(done[3])
        last = work((2,), after(chunk(2, *ties), halves[3]))
    halves[2] = halve(last)
    for slot in (1, 0):
        halves[slot] = halve(done[slot])

    own = rows.shape[0]
    back = {}
    for slot, ties in ((3, []), (2, []), (1, [3]), (0, [2])):
        away = after(halves[slot][own:], *[back[t] for t in ties], *([halves[2]] if ties else []))
        back[slot] = ring.across(away, top)
    sums = plane_sums(ring, lambda slot: add(halves[slot][:own], back[slot]))
    return sums, [crossed[1], crossed[2], back[2]]


def other_half(ring, weight, groups, ties):
    top = ring.bits[0]
    rows = weight.shape[0] // 2
    odd = lax.axis_index("groups") % 2
    pieces = []
    for piece, (begin, swap) in enumerate(ties):
        if groups % 2:
            pieces.append(ring.across(after(weight[piece * rows : (piece + 1) * rows], *begin), top))
            continue
        sent = lax.dynamic_slice_in_dim(weight, piece * rows + odd * (rows // 2), rows // 2, axis=0)
        here = after(ring.across(after(sent, *begin), top), *swap)
        there = lax.ppermute(here, "groups", [(g, g ^ 1) for g in range(groups)])
        pieces += [jnp.where(odd == 0, here, there), jnp.where(odd == 0, there, here)]
    return jnp.concatenate(pieces, axis=0)


def plane_weight(ring, weight, other):
    held = jnp.where(ring.high(ring.bits[0]), jnp.stack([other, weight]), jnp.stack([weight, other]))
    for i, bit in enumerate(ring.bits[1:]):
        other = ring.across(held, bit)
        axis = i + 1
        held = jnp.where(ring.high(bit), jnp.stack([other, held], axis), jnp.stack([held, other], axis))
    return held.reshape(ring.plane * weight.shape[0], weight.shape[1])


def merge(ring, merged_in, weight):
    share = merged_in.shape[1] // PLANES
    products = {}
    for slot in (2, 3, 1, 0):
        piece = lax.dynamic_slice_in_dim(merged_in, (ring.z ^ slot) * share, share, axis=1)
        products[slot] = jnp.dot(ring.between(piece, slot), weight, preferred_element_type=jnp.float32)
        if slot:
            products[slot] = products[slot].astype(jnp.bfloat16)
    return plane_sums(ring, lambda slot: products[slot])


def local(
    hidden_rows,
    token_embed,
    first_routes,
    first_gates,
    first_gate_up,
    first_down,
    second_routes,
    second_gates,
    second_gate_up,
    second_down,
    hidden_gain,
    embed_gain,
    merge_weight,
):
    ring = Ring()
    width = hidden_rows.shape[1]
    lanes = gate_lanes([(first_routes, first_gates), (second_routes, second_gates)])
    top = first_routes.shape[1]
    people = (ring.me, ring.me ^ 1)
    second_lanes = {}

    def first_work(slots, chunk):
        lanes = chunk[:, width:]
        second_lanes[slots[0]] = lanes[: chunk.shape[0] // 2]
        return experts(
            chunk[:, :width], [gate_column(lanes, ring.me, 0, top)], [(first_gate_up[0], first_down[0])]
        )

    def second_work(slots, chunk):
        lanes = jnp.concatenate([second_lanes[slot] for slot in slots], axis=0)
        return experts(chunk, [gate_column(lanes, who, 1, top) for who in people], second_pair)

    first, steps = routed(ring, jnp.concatenate([hidden_rows, lanes], axis=1), first_work, False)
    mine = (second_gate_up[0], second_down[0])
    second_pair = (mine, tuple(ring.across(after(w, steps[1]), ring.bits[-1]) for w in mine))
    ties = [([], [steps[0]]), ([steps[1]], [steps[2]])]
    weight = plane_weight(ring, merge_weight, other_half(ring, merge_weight, lax.axis_size("groups"), ties))
    after_first = (hidden_rows.astype(jnp.float32) + first).astype(jnp.bfloat16)
    merged_in = jnp.concatenate([normed(after_first, hidden_gain), normed(token_embed, embed_gain)], axis=1)
    merged = merge(ring, merged_in, weight)
    after_merge = (after_first.astype(jnp.float32) + jax.nn.silu(merged)).astype(jnp.bfloat16)
    second, _ = routed(ring, after(after_merge, *second_pair[1]), second_work, True)
    return (after_merge.astype(jnp.float32) + second).astype(jnp.bfloat16)


def solution(mesh):
    rows = P(("groups", "inner"), None)
    weight = P("inner", None, None)
    return jax.shard_map(
        local,
        mesh=mesh,
        in_specs=(rows, rows, rows, rows, weight, weight, rows, rows, weight, weight, P(), P(), P("inner", None)),
        out_specs=rows,
        check_vma=False,
    )
```

```python
import jax
import jax.numpy as jnp
from jax import lax
from jax.sharding import PartitionSpec as P

EPSILON = 1e-06
PLANES = 4


class Ring:
    def __init__(self):
        self.size = lax.axis_size("inner")
        self.plane = self.size // PLANES
        self.me = lax.axis_index("inner")
        self.z = self.me // self.plane
        self.inside = (self.z == 1) | (self.z == 2)
        self.bits = []
        bit = self.plane // 2
        while bit:
            self.bits.append(bit)
            bit //= 2

    def send(self, values, pairs):
        perm = [(a * self.plane + i, b * self.plane + i) for a, b in pairs for i in range(self.plane)]
        return lax.ppermute(values, "inner", perm)

    def between(self, values, slot):
        return self.send(values, [(p, p ^ slot) for p in range(PLANES)]) if slot else values

    def across(self, values, bit):
        return lax.ppermute(values, "inner", [(d, d ^ bit) for d in range(self.size)])

    def high(self, bit):
        return (self.me // bit) % 2 == 1


def after(values, *others):
    return lax.optimization_barrier((values, *others))[0]


def add(*terms):
    return sum(t.astype(jnp.float32) for t in terms).astype(jnp.bfloat16)


def within_plane(ring, chunk, bits):
    for bit in reversed(bits):
        rows = chunk.shape[0] // 2
        chunk = add(chunk[:rows], ring.across(chunk[rows:], bit))
    return chunk


def plane_sums(ring, part):
    return sum(ring.between(part(slot), slot).astype(jnp.float32) for slot in (0, 3, 2, 1))


def gate_lanes(layers):
    pieces = []
    for routes, gates in layers:
        high = gates.astype(jnp.bfloat16).astype(jnp.float32)
        pieces += [routes.astype(jnp.float32), high, gates - high]
    top = pieces[0].shape[1]
    width = -(-top * len(pieces) // 128) * 128
    placed = [jnp.pad(p, ((0, 0), (i * top, width - (i + 1) * top))) for i, p in enumerate(pieces)]
    return sum(placed).astype(jnp.bfloat16)


def gate_column(lanes, who, layer, top):
    named, high, low = (lanes[:, (3 * layer + i) * top :][:, :top].astype(jnp.float32) for i in range(3))
    return jnp.sum(jnp.where(named == who.astype(jnp.float32), high + low, 0.0), axis=1, keepdims=True)


def normed(values, gain):
    widened = values.astype(jnp.float32)
    inverse = lax.rsqrt(jnp.mean(widened * widened, axis=-1, keepdims=True) + EPSILON)
    return (widened * inverse * gain).astype(jnp.bfloat16)


def experts(rows, gates, weights):
    total = 0.0
    for gate, (gate_up, down) in zip(gates, weights):
        width = down.shape[0]
        projected = jnp.dot(rows, gate_up, preferred_element_type=jnp.float32)
        hidden = jax.nn.silu(projected[:, :width]) * projected[:, width:] * gate
        total = total + jnp.dot(hidden.astype(jnp.bfloat16), down, preferred_element_type=jnp.float32)
    return total.astype(jnp.bfloat16)


def routed(ring, rows, work, paired):
    top = ring.bits[0]
    below = ring.bits[1:-1] if paired else ring.bits[1:]
    columns = {0: rows}
    for slot in (1, 3, 2):
        columns[slot] = ring.between(rows, slot)
    crossed = {0: ring.across(rows, top)}
    crossed[1] = ring.across(after(columns[1], crossed[0]) if paired else columns[1], top)
    crossed[3] = ring.across(after(columns[3], crossed[1]), top)
    crossed[2] = ring.across(after(columns[2], crossed[3]), top)

    def chunk(slot, *ties):
        part = after(jnp.concatenate([columns[slot], crossed[slot]], axis=0), *ties)
        for bit in below:
            part = jnp.concatenate([part, ring.across(part, bit)], axis=0)
        return part

    def halve(done):
        return within_plane(ring, done, below)

    halves = {}
    if paired:
        both = work((3, 0), after(jnp.concatenate([chunk(3), chunk(0)], axis=0), crossed[3]))
        count = both.shape[0] // 2
        halves[3] = halve(both[:count])
        done = {0: both[count:], 1: work((1,), after(chunk(1), both))}
        last = work((2,), after(chunk(2), done[1], halves[3]))
    else:
        done = {}
        ties = [crossed[3]]
        for slot in (0, 1, 3):
            done[slot] = work((slot,), after(chunk(slot), *ties))
            ties = [done[slot]]
        halves[3] = halve(done[3])
        last = work((2,), after(chunk(2, *ties), halves[3]))
    halves[2] = halve(last)
    for slot in (1, 0):
        halves[slot] = halve(done[slot])

    own = rows.shape[0]
    back = {}
    for slot, ties in ((3, []), (2, []), (1, [3]), (0, [2])):
        away = after(halves[slot][own:], *[back[t] for t in ties], *([halves[2]] if ties else []))
        back[slot] = ring.across(away, top)
    sums = plane_sums(ring, lambda slot: add(halves[slot][:own], back[slot]))
    return sums, [crossed[1], crossed[2], back[2]]


def other_half(ring, weight, groups, ties):
    top = ring.bits[0]
    rows = weight.shape[0] // 2
    odd = lax.axis_index("groups") % 2
    pieces = []
    for piece, (begin, swap) in enumerate(ties):
        if groups % 2:
            pieces.append(ring.across(after(weight[piece * rows : (piece + 1) * rows], *begin), top))
            continue
        sent = lax.dynamic_slice_in_dim(weight, piece * rows + odd * (rows // 2), rows // 2, axis=0)
        here = after(ring.across(after(sent, *begin), top), *swap)
        there = lax.ppermute(here, "groups", [(g, g ^ 1) for g in range(groups)])
        pieces += [jnp.where(odd == 0, here, there), jnp.where(odd == 0, there, here)]
    return jnp.concatenate(pieces, axis=0)


def plane_weight(ring, weight, other):
    held = jnp.where(ring.high(ring.bits[0]), jnp.stack([other, weight]), jnp.stack([weight, other]))
    for i, bit in enumerate(ring.bits[1:]):
        other = ring.across(held, bit)
        axis = i + 1
        held = jnp.where(ring.high(bit), jnp.stack([other, held], axis), jnp.stack([held, other], axis))
    return held.reshape(ring.plane * weight.shape[0], weight.shape[1])


def merge(ring, merged_in, weight):
    share = merged_in.shape[1] // PLANES
    products = {}
    for slot in (2, 3, 1, 0):
        piece = lax.dynamic_slice_in_dim(merged_in, (ring.z ^ slot) * share, share, axis=1)
        products[slot] = jnp.dot(ring.between(piece, slot), weight, preferred_element_type=jnp.float32)
        if slot:
            products[slot] = products[slot].astype(jnp.bfloat16)
    return plane_sums(ring, lambda slot: products[slot])


def local(
    hidden_rows,
    token_embed,
    first_routes,
    first_gates,
    first_gate_up,
    first_down,
    second_routes,
    second_weights,
    second_gate_up,
    second_down,
    hidden_gain,
    embed_gain,
    merge_weight,
):
    ring = Ring()
    width = hidden_rows.shape[1]
    lanes = gate_lanes([(first_routes, first_gates), (second_routes, second_weights)])
    top = first_routes.shape[1]
    people = (ring.me, ring.me ^ 1)
    second_gates = {}

    def first_work(slots, chunk):
        lanes = chunk[:, width:]
        paired = lanes[: chunk.shape[0] // 2]
        second_gates[slots[0]] = [gate_column(paired, who, 1, top) for who in people]
        return experts(
            chunk[:, :width], [gate_column(lanes, ring.me, 0, top)], [(first_gate_up[0], first_down[0])]
        )

    def second_work(slots, chunk):
        gates = [jnp.concatenate([second_gates[slot][i] for slot in slots], axis=0) for i in range(2)]
        return experts(chunk, gates, second_pair)

    first, steps = routed(ring, jnp.concatenate([hidden_rows, lanes], axis=1), first_work, False)
    mine = (second_gate_up[0], second_down[0])
    second_pair = (mine, tuple(ring.across(after(w, steps[1]), ring.bits[-1]) for w in mine))
    ties = [([], [steps[0]]), ([steps[1]], [steps[2]])]
    weight = plane_weight(ring, merge_weight, other_half(ring, merge_weight, lax.axis_size("groups"), ties))
    after_first = (hidden_rows.astype(jnp.float32) + first).astype(jnp.bfloat16)
    merged_in = jnp.concatenate([normed(after_first, hidden_gain), normed(token_embed, embed_gain)], axis=1)
    merged = merge(ring, merged_in, after(weight, *[g for slot in range(PLANES) for g in second_gates[slot]]))
    after_merge = (after_first.astype(jnp.float32) + jax.nn.silu(merged)).astype(jnp.bfloat16)
    second, _ = routed(ring, after(after_merge, *second_pair[1]), second_work, True)
    return (after_merge.astype(jnp.float32) + second).astype(jnp.bfloat16)


def solution(mesh):
    rows = P(("groups", "inner"), None)
    weight = P("inner", None, None)
    return jax.shard_map(
        local,
        mesh=mesh,
        in_specs=(rows, rows, rows, rows, weight, weight, rows, rows, weight, weight, P(), P(), P("inner", None)),
        out_specs=rows,
        check_vma=False,
    )
```

```python
import jax
import jax.numpy as jnp
from jax import lax
from jax.sharding import PartitionSpec as P

EPSILON = 1e-06
PLANES = 4


class Ring:
    def __init__(self):
        self.size = lax.axis_size("inner")
        self.plane = self.size // PLANES
        self.me = lax.axis_index("inner")
        self.z = self.me // self.plane
        self.inside = (self.z == 1) | (self.z == 2)
        self.bits = []
        bit = self.plane // 2
        while bit:
            self.bits.append(bit)
            bit //= 2

    def send(self, values, pairs):
        perm = [(a * self.plane + i, b * self.plane + i) for a, b in pairs for i in range(self.plane)]
        return lax.ppermute(values, "inner", perm)

    def between(self, values, slot):
        return self.send(values, [(p, p ^ slot) for p in range(PLANES)]) if slot else values

    def across(self, values, bit):
        return lax.ppermute(values, "inner", [(d, d ^ bit) for d in range(self.size)])

    def high(self, bit):
        return (self.me // bit) % 2 == 1


def after(values, *others):
    return lax.optimization_barrier((values, *others))[0]


def add(*terms):
    return sum(t.astype(jnp.float32) for t in terms).astype(jnp.bfloat16)


def within_plane(ring, chunk, bits):
    for bit in reversed(bits):
        rows = chunk.shape[0] // 2
        chunk = add(chunk[:rows], ring.across(chunk[rows:], bit))
    return chunk


def plane_sums(ring, part):
    return sum(ring.between(part(slot), slot).astype(jnp.float32) for slot in (0, 3, 2, 1))


def gate_lanes(layers):
    pieces = []
    for routes, gates in layers:
        high = gates.astype(jnp.bfloat16).astype(jnp.float32)
        pieces += [routes.astype(jnp.float32), high, gates - high]
    top = pieces[0].shape[1]
    width = -(-top * len(pieces) // 128) * 128
    placed = [jnp.pad(p, ((0, 0), (i * top, width - (i + 1) * top))) for i, p in enumerate(pieces)]
    return sum(placed).astype(jnp.bfloat16)


def gate_column(lanes, who, layer, top):
    named, high, low = (lanes[:, (3 * layer + i) * top :][:, :top].astype(jnp.float32) for i in range(3))
    return jnp.sum(jnp.where(named == who.astype(jnp.float32), high + low, 0.0), axis=1, keepdims=True)


def normed(values, gain):
    widened = values.astype(jnp.float32)
    inverse = lax.rsqrt(jnp.mean(widened * widened, axis=-1, keepdims=True) + EPSILON)
    return (widened * inverse * gain).astype(jnp.bfloat16)


def experts(rows, gates, weights):
    total = 0.0
    for gate, (gate_up, down) in zip(gates, weights):
        width = down.shape[0]
        projected = jnp.dot(rows, gate_up, preferred_element_type=jnp.float32)
        hidden = jax.nn.silu(projected[:, :width]) * projected[:, width:] * gate
        total = total + jnp.dot(hidden.astype(jnp.bfloat16), down, preferred_element_type=jnp.float32)
    return total.astype(jnp.bfloat16)


def routed(ring, rows, work, paired):
    top = ring.bits[0]
    below = ring.bits[1:-1] if paired else ring.bits[1:]
    columns = {0: rows}
    for slot in (1, 3, 2):
        columns[slot] = ring.between(rows, slot)
    crossed = {0: ring.across(rows, top)}
    crossed[1] = ring.across(after(columns[1], crossed[0]) if paired else columns[1], top)
    crossed[3] = ring.across(after(columns[3], crossed[1]), top)
    crossed[2] = ring.across(after(columns[2], crossed[3]), top)

    def chunk(slot, *ties):
        part = after(jnp.concatenate([columns[slot], crossed[slot]], axis=0), *ties)
        for bit in below:
            part = jnp.concatenate([part, ring.across(part, bit)], axis=0)
        return part

    def halve(done):
        return within_plane(ring, done, below)

    halves = {}
    if paired:
        both = work((3, 0), after(jnp.concatenate([chunk(3), chunk(0)], axis=0), crossed[3]))
        count = both.shape[0] // 2
        halves[3] = halve(both[:count])
        done = {0: both[count:], 1: work((1,), after(chunk(1), both))}
        last = work((2,), after(chunk(2), done[1], halves[3]))
    else:
        done = {}
        ties = [crossed[3]]
        for slot in (0, 1, 3):
            done[slot] = work((slot,), after(chunk(slot), *ties))
            ties = [done[slot]]
        halves[3] = halve(done[3])
        early = ring.across(halves[3][rows.shape[0] :], top)
        last = work((2,), after(chunk(2, *ties), early))
    halves[2] = halve(last)
    for slot in (1, 0):
        halves[slot] = halve(done[slot])

    own = rows.shape[0]
    back = {}
    for slot, ties in ((3, []), (2, []), (1, [3]), (0, [2])):
        if slot == 3 and not paired:
            back[slot] = early
            continue
        away = after(halves[slot][own:], *[back[t] for t in ties], *([halves[2]] if ties else []))
        back[slot] = ring.across(away, top)
    sums = plane_sums(ring, lambda slot: add(halves[slot][:own], back[slot]))
    return sums, [crossed[1], crossed[2], back[3], back[2]]


def other_half(ring, weight, groups, ties):
    top = ring.bits[0]
    rows = weight.shape[0] // 2
    odd = lax.axis_index("groups") % 2
    pieces = []
    for piece, (begin, swap) in enumerate(ties):
        if groups % 2:
            pieces.append(ring.across(after(weight[piece * rows : (piece + 1) * rows], *begin), top))
            continue
        sent = lax.dynamic_slice_in_dim(weight, piece * rows + odd * (rows // 2), rows // 2, axis=0)
        here = after(ring.across(after(sent, *begin), top), *swap)
        there = lax.ppermute(here, "groups", [(g, g ^ 1) for g in range(groups)])
        pieces += [jnp.where(odd == 0, here, there), jnp.where(odd == 0, there, here)]
    return jnp.concatenate(pieces, axis=0)


def plane_weight(ring, weight, other):
    held = jnp.where(ring.high(ring.bits[0]), jnp.stack([other, weight]), jnp.stack([weight, other]))
    for i, bit in enumerate(ring.bits[1:]):
        other = ring.across(held, bit)
        axis = i + 1
        held = jnp.where(ring.high(bit), jnp.stack([other, held], axis), jnp.stack([held, other], axis))
    return held.reshape(ring.plane * weight.shape[0], weight.shape[1])


def merge(ring, merged_in, weight):
    share = merged_in.shape[1] // PLANES
    products = {}
    for slot in (2, 3, 1, 0):
        piece = lax.dynamic_slice_in_dim(merged_in, (ring.z ^ slot) * share, share, axis=1)
        products[slot] = jnp.dot(ring.between(piece, slot), weight, preferred_element_type=jnp.float32)
        if slot:
            products[slot] = products[slot].astype(jnp.bfloat16)
    return plane_sums(ring, lambda slot: products[slot])


def local(
    hidden_rows,
    token_embed,
    first_routes,
    first_gates,
    first_gate_up,
    first_down,
    second_routes,
    second_gates,
    second_gate_up,
    second_down,
    hidden_gain,
    embed_gain,
    merge_weight,
):
    ring = Ring()
    width = hidden_rows.shape[1]
    lanes = gate_lanes([(first_routes, first_gates), (second_routes, second_gates)])
    top = first_routes.shape[1]
    people = (ring.me, ring.me ^ 1)
    second_lanes = {}

    def first_work(slots, chunk):
        lanes = chunk[:, width:]
        second_lanes[slots[0]] = lanes[: chunk.shape[0] // 2]
        return experts(
            chunk[:, :width], [gate_column(lanes, ring.me, 0, top)], [(first_gate_up[0], first_down[0])]
        )

    def second_work(slots, chunk):
        lanes = jnp.concatenate([second_lanes[slot] for slot in slots], axis=0)
        return experts(chunk, [gate_column(lanes, who, 1, top) for who in people], second_pair)

    first, steps = routed(ring, jnp.concatenate([hidden_rows, lanes], axis=1), first_work, False)
    mine = (second_gate_up[0], second_down[0])
    second_pair = (mine, tuple(ring.across(after(w, steps[1]), ring.bits[-1]) for w in mine))
    ties = [([], [steps[0]]), ([steps[2]], [steps[3]])]
    weight = plane_weight(ring, merge_weight, other_half(ring, merge_weight, lax.axis_size("groups"), ties))
    after_first = (hidden_rows.astype(jnp.float32) + first).astype(jnp.bfloat16)
    merged_in = jnp.concatenate([normed(after_first, hidden_gain), normed(token_embed, embed_gain)], axis=1)
    merged = merge(ring, merged_in, weight)
    after_merge = (after_first.astype(jnp.float32) + jax.nn.silu(merged)).astype(jnp.bfloat16)
    second, _ = routed(ring, after(after_merge, *second_pair[1]), second_work, True)
    return (after_merge.astype(jnp.float32) + second).astype(jnp.bfloat16)


def solution(mesh):
    rows = P(("groups", "inner"), None)
    weight = P("inner", None, None)
    return jax.shard_map(
        local,
        mesh=mesh,
        in_specs=(rows, rows, rows, rows, weight, weight, rows, rows, weight, weight, P(), P(), P("inner", None)),
        out_specs=rows,
        check_vma=False,
    )
```
